128 devices in a mesh: section: 4 (over y), seq: 32 (over z, x, core).
Axes of the slice: x: 4, y: 4, z: 4, core: 2. Of those that a mesh axis runs over, the one named last changes fastest.
Arguments:
- patch_in: bfloat16 [4, 2, 2048, 2432], P('section', None, 'seq'), may hold values from -6 to 6
- modulation: float32 [4, 3, 2432], P('section'), may hold values from -3 to 3
- qkv_weight: bfloat16 [4, 2432, 6144], P('section', None, 'seq'), may hold values from -0.125 to 0.125
- qk_gain: float32 [4, 2, 64], P('section'), may hold values from 0.1 to 1.9
- out_weight: bfloat16 [4, 2048, 2432], P('section'), may hold values from -0.125 to 0.125
- kv_cache: bfloat16 [4, 2, 8192, 4096], P('section', None, None, 'seq'), may hold values from -190 to 190
- text_kv: bfloat16 [4, 2, 256, 4096], P('section', None, None, 'seq'), may hold values from -6 to 6
- patch_offsets: int32 [4], replicated, may hold values from 0 to 6144, as said below
- step_index: int32 [1], replicated, may hold values from 0 to 3
- text_count: int32 [2], replicated, may hold values from 64 to 256, as said below
Outputs:
- patch_out: bfloat16 [4, 2, 2048, 2432], P('section', None, 'seq')
- fresh_kv: bfloat16 [4, 2, 2048, 4096], P('section', None, None, 'seq')
The draws below stay inside these ranges and needn't reach their ends.
Inputs may be any that keep to these rules, and one draw needn't show every extreme that they name: `patch_offsets`: a permutation of the multiples of 2048 below 8192. `text_count`: in every draw one of the two branches uses all 256 text slots.
All inputs are finite; a program needn't handle non-finite values.
Results may differ from the reference program's by a relative error of at most 0.0017.
The reference program's roundings to bfloat16 on the way count: a program that leaves them out, or rounds other values in their place, can miss the bound.
Values may be sent and summed in bfloat16 or wider, within the bound.
No kernel may reach another device: no remote copies, remote signals or barrier semaphores. Data moves between devices by JAX's collectives and lax.ppermute only.
A program may use at most 128 MiB of HBM per device.

```python
import math
import jax
import jax.numpy as jnp
from jax import lax

D = 2432
HD = 64
HEADS = 32
PATCHES = 4
TEXT = 256
PATCH_TOK = 2048
IMG = 8192
N_SECTION = 4


def draw_kv_cache(key, part):
    key = jax.random.fold_in(key, 11)
    key_base = jax.random.fold_in(key, 0)
    key_value = jax.random.fold_in(key, 3)
    shape_full = (N_SECTION, 2, IMG, HEADS, HD)
    keys_part = 1.5 * jnp.clip(jax.random.normal(key_base, shape_full, jnp.float32), -6.0, 6.0)
    values_part = jnp.clip(jax.random.normal(key_value, shape_full, jnp.float32), -6.0, 6.0)
    joined = jnp.stack([keys_part, values_part], axis=4)
    return joined.reshape(N_SECTION, 2, IMG, HEADS * 2 * HD).astype(jnp.bfloat16)


def draw_patch_offsets(key, part):
    key = jax.random.fold_in(key, 7)
    order = jax.random.permutation(key, PATCHES)
    return (order * PATCH_TOK).astype(jnp.int32)


def draw_text_count(key, part):
    key = jax.random.fold_in(key, 5)
    key_which, key_other = jax.random.split(key)
    which_branch = jax.random.randint(key_which, (), 0, 2)
    other_count = jax.random.randint(key_other, (), TEXT // 4, TEXT + 1)
    return jnp.where(jnp.arange(2) == which_branch, TEXT, other_count).astype(jnp.int32)


def level_of(key, shape, cuts, least, largest):
    def one(position, shards_of):
        draws = jax.random.uniform(jax.random.fold_in(jax.random.fold_in(key, 6), position), (shards_of,), jnp.float32, least / len(cuts), largest / len(cuts))
        return jnp.repeat(jnp.exp(draws), shape[position] // shards_of).reshape((-1,) + (1,) * (len(shape) - position - 1))

    loudness = one(*cuts[0])
    for cut in cuts[1:]:
        loudness = loudness * one(*cut)
    return loudness


def normal_values(own_key, extent, width, reach, shards=(), kind=jnp.bfloat16):
    values = jax.random.normal(own_key, extent, jnp.float32) * width
    if len(shards) > 0:
        values = level_of(own_key, extent, shards, -0.22, 0.18) * values
    return jnp.clip(values, min=-reach, max=reach).astype(kind)


def setup_inputs(seed: int = 0) -> dict:
    seeds = jax.random.split(jax.random.key(seed), 11)
    return {
        "patch_in": normal_values(seeds[0], (N_SECTION, 2, PATCH_TOK, D), 1.0, 6.0, ((0, 4), (2, 32))),
        "modulation": normal_values(seeds[1], (N_SECTION, 3, D), 0.5, 3.0, ((0, 4),), jnp.float32),
        "qkv_weight": normal_values(seeds[2], (N_SECTION, D, 3 * HEADS * HD), D ** -0.5, 0.125, ((0, 4), (2, 32))),
        "qk_gain": jnp.clip(1.0 + 0.18 * jax.random.normal(seeds[3], (N_SECTION, 2, HD), jnp.float32), 0.1, 1.9),
        "out_weight": normal_values(seeds[4], (N_SECTION, HEADS * HD, D), (HEADS * HD) ** -0.5, 0.125, ((0, 4),)),
        "kv_cache": draw_kv_cache(jax.random.fold_in(seeds[10], 71), 0),
        "text_kv": normal_values(seeds[6], (N_SECTION, 2, TEXT, HEADS * 2 * HD), 1.0, 6.0, ((0, 4), (3, 32))),
        "patch_offsets": draw_patch_offsets(jax.random.fold_in(seeds[10], 71), 0),
        "step_index": jax.random.randint(seeds[8], (1,), 0, PATCHES).astype(jnp.int32),
        "text_count": draw_text_count(jax.random.fold_in(seeds[10], 71), 0),
    }


def modulated(entering, mod_rows):
    values = entering.astype(jnp.float32)
    center = lax.optimization_barrier(jnp.mean(values, axis=-1, keepdims=True))
    spread = lax.optimization_barrier(jnp.mean((values - center) ** 2, axis=-1, keepdims=True))
    normal_rows = (values - center) * lax.rsqrt(spread + 1e-06)
    return (normal_rows * (1.0 + mod_rows[1]) + mod_rows[0]).astype(jnp.bfloat16)

def normalize_heads(projected, gains):
    head_size = gains.shape[-1]
    shaped = projected.reshape(projected.shape[0], projected.shape[1], -1, 3, head_size)
    queries = shaped[:, :, :, 0, :]
    keys_new = shaped[:, :, :, 1, :]
    values_new = shaped[:, :, :, 2, :]
    queries = queries * lax.rsqrt(lax.optimization_barrier(jnp.mean(queries * queries, axis=-1, keepdims=True)) + 1e-06) * gains[0]
    keys_new = keys_new * lax.rsqrt(lax.optimization_barrier(jnp.mean(keys_new * keys_new, axis=-1, keepdims=True)) + 1e-06) * gains[1]
    joined = jnp.stack([queries, keys_new, values_new], axis=3).astype(jnp.bfloat16)
    return joined.reshape(projected.shape)

def attend(mixed, cache, text_part, offset, counts):
    batch, rows_all, packed = mixed.shape
    heads_here = packed // (3 * HD)
    shaped = mixed.reshape(batch, rows_all, heads_here, 3, HD)
    fresh = shaped[:, :, :, 1:, :].reshape(batch, rows_all, heads_here * 2 * HD)
    zero_index = jnp.zeros((), jnp.int32)
    keys_image = lax.dynamic_update_slice(cache, fresh, (zero_index, offset.astype(jnp.int32), zero_index))
    every_key = jnp.concatenate([keys_image, text_part], axis=1)
    key_count = every_key.shape[1]
    image_rows = cache.shape[1]
    every_key = every_key.reshape(batch, key_count, heads_here, 2, HD)
    key_vecs = every_key[:, :, :, 0, :].astype(jnp.float32)
    value_vecs = every_key[:, :, :, 1, :].astype(jnp.float32)
    positions = jnp.arange(key_count, dtype=jnp.int32)
    usable = (positions[None, :] < image_rows) | (positions[None, :] - image_rows < counts[:, None])
    block_rows = math.gcd(rows_all, 512)
    blocks = rows_all // block_rows
    queries = shaped[:, :, :, 0, :].reshape(batch, blocks, block_rows, heads_here, HD).transpose(1, 0, 2, 3, 4)

    def block_attend(query_block):
        scores = jnp.einsum('bqhd,bkhd->bhqk', query_block.astype(jnp.float32), key_vecs) * HD ** (-0.5)
        scores = jnp.where(usable[:, None, None, :], scores, -1e+30)
        highest = lax.optimization_barrier(jnp.max(scores, axis=-1, keepdims=True))
        raised = jnp.exp(scores - highest)
        totals = lax.optimization_barrier(jnp.sum(raised, axis=-1, keepdims=True))
        probs = (raised / totals).astype(jnp.bfloat16)
        result = jnp.einsum('bhqk,bkhd->bqhd', probs.astype(jnp.float32), value_vecs)
        return result.astype(jnp.bfloat16)
    attended = lax.map(block_attend, queries)
    attended = attended.transpose(1, 0, 2, 3, 4).reshape(batch, rows_all, heads_here * HD)
    return (attended, fresh)

def reference(patch_in, modulation, qkv_weight, qk_gain, out_weight, kv_cache, text_kv, patch_offsets, step_index, text_count):
    section_outputs = []
    section_fresh = []
    for section_number in range(N_SECTION):
        patch_number = (step_index[0] - section_number) % PATCHES
        offset = patch_offsets[patch_number]
        entering = patch_in[section_number]
        normed = modulated(entering, modulation[section_number])
        projected = jnp.dot(normed.reshape(2 * PATCH_TOK, D), qkv_weight[section_number], preferred_element_type=jnp.float32)
        mixed = normalize_heads(projected.reshape(2, PATCH_TOK, 3 * HEADS * HD), qk_gain[section_number])
        head_mixed = mixed.reshape(2, PATCH_TOK, HEADS, 3 * HD).transpose(2, 0, 1, 3)
        head_cache = kv_cache[section_number].reshape(2, IMG, HEADS, 2 * HD).transpose(2, 0, 1, 3)
        head_text = text_kv[section_number].reshape(2, TEXT, HEADS, 2 * HD).transpose(2, 0, 1, 3)

        def per_head(items):
            return attend(items[0], items[1], items[2], offset, text_count)
        attended, fresh = lax.map(per_head, (head_mixed, head_cache, head_text))
        attended = attended.transpose(1, 2, 0, 3).reshape(2 * PATCH_TOK, HEADS * HD)
        fresh = fresh.transpose(1, 2, 0, 3).reshape(2, PATCH_TOK, HEADS * 2 * HD)
        projected_out = jnp.dot(attended, out_weight[section_number], preferred_element_type=jnp.float32)
        block_out = entering.astype(jnp.float32) + modulation[section_number, 2] * projected_out.reshape(2, PATCH_TOK, D)
        section_outputs.append(block_out.astype(jnp.bfloat16))
        section_fresh.append(fresh)
    patch_out = jnp.roll(jnp.stack(section_outputs, axis=0), 1, axis=0)
    return (patch_out, jnp.stack(section_fresh, axis=0))
```

```python
import functools
import math

import jax
import jax.numpy as jnp
from jax import lax
from jax.experimental import pallas as pl
from jax.experimental.pallas import tpu as pltpu
from jax.sharding import PartitionSpec as P

HD = 64
SIDE = 4
CHIPS = SIDE * SIDE
STEPS = (0, 1, -1, 2)
MIB = 2**20


def pairs_of(phase, step):
    pairs = []
    for z in range(SIDE):
        for x in range(SIDE):
            for core in range(2):
                if (phase + core) % 2 == 0:
                    to = (z * SIDE + (x + step) % SIDE) * 2 + core
                else:
                    to = (((z + step) % SIDE) * SIDE + x) * 2 + core
                pairs.append(((z * SIDE + x) * 2 + core, to))
    return pairs


def along(value, phase, step):
    return lax.ppermute(value, "seq", pairs_of(phase, step))


def swapped(value):
    return lax.ppermute(value, "seq", [(i, i ^ 1) for i in range(2 * CHIPS)])


def after(value, *others):
    return lax.optimization_barrier((value, *others))[0]


def norm_kernel(x_ref, mod_ref, first_ref, second_ref):
    shift = mod_ref[0:1, :]
    scale = 1.0 + mod_ref[1:2, :]
    for branch, out_ref in enumerate((first_ref, second_ref)):
        values = x_ref[branch].astype(jnp.float32)
        center = jnp.mean(values, axis=-1, keepdims=True)
        moved = values - center
        spread = jnp.mean(moved * moved, axis=-1, keepdims=True)
        out_ref[...] = (moved * lax.rsqrt(spread + 1e-06) * scale + shift).astype(jnp.bfloat16)


def normed_rows(entering, mod_rows):
    rows, width = entering.shape[1:]
    out = jax.ShapeDtypeStruct((rows, width), jnp.bfloat16)
    return pl.pallas_call(
        norm_kernel,
        out_shape=(out, out),
        compiler_params=pltpu.CompilerParams(vmem_limit_bytes=16 * MIB),
    )(entering, mod_rows)


def project_kernel(*refs):
    pieces = refs[:-8]
    own_w, other_w, gains, own_q, own_kv, other_q, other_kv, packed = refs[-8:]
    for part, weight in ((0, own_w), (256, other_w)):
        packed[part : part + 2 * HD, :] = weight[HD:, :]
        packed[part + 2 * HD : part + 3 * HD, :] = weight[:HD, :]
        packed[part + 3 * HD : part + 256, :] = jnp.zeros((HD, packed.shape[1]), packed.dtype)
    lane = lax.broadcasted_iota(jnp.int32, (1, 2 * HD), 1)
    query_gain = gains[0:1, :]
    key_gain = gains[1:2, :]
    row = 0
    for piece in pieces:
        rows = piece.shape[0]
        for part, q_ref, kv_ref in ((0, own_q, own_kv), (256, other_q, other_kv)):
            out = lax.dot_general(
                piece[...],
                packed[part : part + 256, :],
                (((1,), (1,)), ((), ())),
                preferred_element_type=jnp.float32,
            )
            kv = out[:, : 2 * HD]
            q = out[:, 2 * HD :]
            key_square = jnp.where(lane < HD, kv * kv, 0.0)
            key_mean = jnp.sum(key_square, axis=-1, keepdims=True) * (1.0 / HD)
            key_scaled = kv * lax.rsqrt(key_mean + 1e-06) * key_gain
            kv_ref[row : row + rows, :] = jnp.where(lane < HD, key_scaled, kv).astype(jnp.bfloat16)
            query_mean = jnp.sum(q * q, axis=-1, keepdims=True) * (1.0 / HD)
            q_ref[row : row + rows, :] = (q * lax.rsqrt(query_mean + 1e-06) * query_gain).astype(
                jnp.bfloat16
            )
        row += rows


def projected_rows(pieces, own_weight, other_weight, gains):
    rows = sum(piece.shape[0] for piece in pieces)
    width = own_weight.shape[1]
    out = jax.ShapeDtypeStruct((rows, 2 * HD), jnp.bfloat16)
    return pl.pallas_call(
        project_kernel,
        out_shape=(out,) * 4,
        scratch_shapes=[pltpu.VMEM((512, width), jnp.bfloat16)],
        compiler_params=pltpu.CompilerParams(vmem_limit_bytes=40 * MIB),
        cost_estimate=pl.CostEstimate(
            flops=2 * rows * width * 512, bytes_accessed=rows * width * 2, transcendentals=0
        ),
    )(*pieces, own_weight, other_weight, gains)


KEY_CHUNK = 2816


def attend_kernel(emit, *refs):
    spots, q_ref, first, second, third, fresh_own, fresh_other, text = refs[:8]
    refs = refs[8:]
    out_ref = refs[0]
    if emit:
        fresh_ref = refs[1]
        refs = refs[1:]
    kaug, kv_all, qaug, e_scr, total_ref = refs[1:]
    rows = q_ref.shape[0]
    keys = kv_all.shape[0]
    half = fresh_own.shape[0]
    text_rows = text.shape[0]
    image = keys - text_rows
    lane = lax.broadcasted_iota(jnp.int32, (1, 2 * HD), 1)
    start = 0
    longest = jnp.zeros((1, 2 * HD), jnp.float32)
    pick = jnp.where(lax.broadcasted_iota(jnp.int32, (2 * HD, 2 * HD), 0) < HD, 1.0, 0.0)
    pick = pick.astype(jnp.bfloat16)
    for source in (first, second, third, fresh_own, fresh_other, text):
        many = source.shape[0]
        kv = source[...]
        kv_all[start : start + many, :] = kv
        wide = kv.astype(jnp.float32)
        turned = pltpu.roll(wide, HD, 1)
        kaug[start : start + many, : 2 * HD] = jnp.where(lane < HD, wide, turned).astype(jnp.bfloat16)
        ones = jnp.where((lane >= HD) & (lane < HD + 3), 1.0, 0.0)
        if start == image:
            used = lax.broadcasted_iota(jnp.int32, (many, 2 * HD), 0) < spots[0]
            ones = jnp.where((lane == HD + 3) & jnp.logical_not(used), -30000.0, ones)
        kaug[start : start + many, 2 * HD :] = jnp.where(lane < HD, wide, ones).astype(jnp.bfloat16)
        lengths = jnp.dot(
            (wide * wide).astype(jnp.bfloat16), pick, preferred_element_type=jnp.float32
        )
        longest = jnp.maximum(longest, jnp.max(lengths, axis=0, keepdims=True))
        start += many
    if emit:
        for block in range(2 * CHIPS):
            here = fresh_own if block < CHIPS else fresh_other
            at = (block % CHIPS) * HD
            to = pl.multiple_of(spots[1 + block] * HD, HD)
            fresh_ref[pl.ds(to, HD), :] = here[at : at + HD, :]

    scaled = q_ref[...].astype(jnp.float32) * (math.log2(math.e) / math.sqrt(HD))
    high = scaled.astype(jnp.bfloat16).astype(jnp.float32)
    left = scaled - high
    middle = left.astype(jnp.bfloat16).astype(jnp.float32)
    low = left - middle
    qaug[:, : 2 * HD] = (high + pltpu.roll(middle, HD, 1)).astype(jnp.bfloat16)

    def lower(bound):
        one = bound.astype(jnp.bfloat16).astype(jnp.float32)
        rest = bound - one
        two = rest.astype(jnp.bfloat16).astype(jnp.float32)
        three = rest - two
        tail = jnp.where(lane == HD, -one, 0.0)
        tail = jnp.where(lane == HD + 1, -two, tail)
        tail = jnp.where(lane == HD + 2, -three, tail)
        tail = jnp.where(lane == HD + 3, 1.0, tail)
        qaug[:, 2 * HD :] = jnp.where(lane < HD, low, tail).astype(jnp.bfloat16)

    def scores(at):
        return lax.dot_general(
            qaug[...],
            kaug[pl.ds(at, KEY_CHUNK), :],
            (((1,), (1,)), ((), ())),
            preferred_element_type=jnp.float32,
        )

    def raise_all():
        def chunk(j, total):
            at = pl.multiple_of(j * KEY_CHUNK, KEY_CHUNK)
            raised = jnp.exp2(scores(at))
            e_scr[:, pl.ds(at, KEY_CHUNK)] = raised
            for part in range(KEY_CHUNK // 128):
                total = total + raised[:, part * 128 : (part + 1) * 128]
            return total

        total = lax.fori_loop(0, keys // KEY_CHUNK, chunk, jnp.zeros((rows, 128), jnp.float32))
        total_ref[...] = jnp.broadcast_to(jnp.sum(total, axis=-1, keepdims=True), (rows, 128))

    size = jnp.sum(scaled * scaled, axis=-1, keepdims=True)
    lower(jnp.sqrt(size * (longest * 1.02)) + 1e-3)
    raise_all()

    @pl.when(jnp.min(total_ref[...]) < 1e-12)
    def _():
        lower(jnp.zeros((rows, 2 * HD), jnp.float32))

        def chunk(j, best):
            found = scores(pl.multiple_of(j * KEY_CHUNK, KEY_CHUNK))
            for part in range(KEY_CHUNK // 128):
                best = jnp.maximum(best, found[:, part * 128 : (part + 1) * 128])
            return best

        best = lax.fori_loop(
            0, keys // KEY_CHUNK, chunk, jnp.full((rows, 128), -3e38, jnp.float32)
        )
        best = jnp.max(best, axis=-1, keepdims=True)
        lower(jnp.broadcast_to(best, (rows, 2 * HD)))
        raise_all()

    share = 1.0 / total_ref[...]

    def weigh(j, sums):
        at = pl.multiple_of(j * KEY_CHUNK, KEY_CHUNK)
        probs = e_scr[:, pl.ds(at, KEY_CHUNK)] * jnp.tile(share, (1, KEY_CHUNK // 128))
        return sums + jnp.dot(
            probs.astype(jnp.bfloat16),
            kv_all[pl.ds(at, KEY_CHUNK), :],
            preferred_element_type=jnp.float32,
        )

    sums = lax.fori_loop(0, keys // KEY_CHUNK, weigh, jnp.zeros((rows, 2 * HD), jnp.float32))
    out_ref[...] = sums[:, HD:].astype(jnp.bfloat16)


def attended_rows(emit, spots, branch, q, cache, fresh_own, fresh_other, text):
    rows = q.shape[0]
    half = fresh_own.shape[0]
    patch = 2 * half
    keys = cache.shape[1] + text.shape[1]
    patches = cache.shape[1] // patch

    def stale(step):
        return pl.BlockSpec(
            (None, patch, 2 * HD),
            lambda i, spots: (branch, lax.rem(spots[1 + 2 * CHIPS] + step, patches), 0),
        )

    def whole(shape):
        return pl.BlockSpec(shape, lambda i, spots: (0, 0))

    out_shape = [jax.ShapeDtypeStruct((rows, HD), jnp.bfloat16)]
    out_specs = [whole((rows, HD))]
    if emit:
        out_shape.append(jax.ShapeDtypeStruct((patch, 2 * HD), jnp.bfloat16))
        out_specs.append(whole((patch, 2 * HD)))
    flops = 4 * rows * keys * 256
    return pl.pallas_call(
        functools.partial(attend_kernel, emit),
        out_shape=out_shape,
        grid_spec=pltpu.PrefetchScalarGridSpec(
            num_scalar_prefetch=1,
            grid=(1,),
            in_specs=[
                whole((rows, 2 * HD)),
                stale(1),
                stale(2),
                stale(3),
                whole((half, 2 * HD)),
                whole((half, 2 * HD)),
                pl.BlockSpec((None, text.shape[1], 2 * HD), lambda i, spots: (branch, 0, 0)),
            ],
            out_specs=out_specs,
            scratch_shapes=[
                pltpu.VMEM((keys, 4 * HD), jnp.bfloat16),
                pltpu.VMEM((keys, 2 * HD), jnp.bfloat16),
                pltpu.VMEM((rows, 4 * HD), jnp.bfloat16),
                pltpu.VMEM((rows, keys), jnp.float32),
                pltpu.VMEM((rows, 128), jnp.float32),
            ],
        ),
        compiler_params=pltpu.CompilerParams(vmem_limit_bytes=56 * MIB),
        cost_estimate=pl.CostEstimate(flops=flops, bytes_accessed=4 * MIB, transcendentals=0),
    )(spots, q, cache, cache, cache, fresh_own, fresh_other, text)


def finish_kernel(order, j0, j1, j2, j3, weight, entering, gate, out_ref, total):
    step = pl.program_id(0)

    @pl.when(step == 0)
    def _():
        total[...] = jnp.zeros_like(total)

    sums = total[...]
    for x in range(SIDE):
        place = order[step * SIDE + x]
        outer = lax.div(place, SIDE)
        inner = lax.rem(place, SIDE)
        lhs = jnp.where(
            outer == 0,
            j0[inner],
            jnp.where(outer == 1, j1[inner], jnp.where(outer == 2, j2[inner], j3[inner])),
        )
        sums = sums + jnp.dot(
            lhs, weight[x * 2 * HD : (x + 1) * 2 * HD, :], preferred_element_type=jnp.float32
        )
    total[...] = sums

    @pl.when(step == SIDE - 1)
    def _():
        out_ref[...] = (entering[...].astype(jnp.float32) + gate[2:3, :] * total[...]).astype(
            jnp.bfloat16
        )


def finished_rows(order, blocks, weight, entering, branch, mod_rows):
    rows, width = entering.shape[1:]
    depth = weight.shape[0] // SIDE
    blocks_spec = pl.BlockSpec((SIDE, rows, 2 * HD), lambda i, order: (0, 0, 0))
    return pl.pallas_call(
        finish_kernel,
        out_shape=jax.ShapeDtypeStruct((rows, width), jnp.bfloat16),
        grid_spec=pltpu.PrefetchScalarGridSpec(
            num_scalar_prefetch=1,
            grid=(SIDE,),
            in_specs=[blocks_spec] * 4
            + [
                pl.BlockSpec((depth, width), lambda i, order: (i, 0)),
                pl.BlockSpec((None, rows, width), lambda i, order: (branch, 0, 0)),
                pl.BlockSpec((3, width), lambda i, order: (0, 0)),
            ],
            out_specs=pl.BlockSpec((rows, width), lambda i, order: (0, 0)),
            scratch_shapes=[pltpu.VMEM((rows, width), jnp.float32)],
        ),
        compiler_params=pltpu.CompilerParams(vmem_limit_bytes=24 * MIB),
        cost_estimate=pl.CostEstimate(
            flops=2 * rows * width * weight.shape[0],
            bytes_accessed=weight.shape[0] * width * 2,
            transcendentals=0,
        ),
    )(order, *blocks, weight, entering, mod_rows)


def gather_first(own):
    rows = own.shape[0]
    left = along(own, 0, 1)
    right = along(own, 0, -1)
    far_low = along(left[: rows // 2], 0, 1)
    far_high = along(right[rows // 2 :], 0, -1)
    return jnp.concatenate([own, left, right, far_low, far_high], axis=0)


def gather_second(line):
    return along(line, 1, 1), along(line, 1, -1)


def gather_third(left, right):
    rows = left.shape[0]
    return along(left[: rows // 2], 1, 1), along(right[rows // 2 :], 1, -1)


def returned(mine, other):
    rows = HD
    both = jnp.concatenate([mine, other], axis=1).reshape(SIDE, SIDE, rows, 2 * HD)
    stage = [both[:, 0]] + [along(both[:, i], 0, -STEPS[i]) for i in (1, 2, 3)]
    stage = jnp.stack(stage, axis=1)
    return [stage[0]] + [along(stage[j], 1, -STEPS[j]) for j in (1, 2, 3)]


def local(
    patch_in,
    modulation,
    qkv_weight,
    qk_gain,
    out_weight,
    kv_cache,
    text_kv,
    patch_offsets,
    step_index,
    text_count,
):
    section_index = lax.axis_index("section")
    place = lax.axis_index("seq")
    core = place % 2
    x = (place // 2) % SIDE
    z = place // (2 * SIDE)
    patch_total = patch_offsets.shape[0]
    patch_number = (step_index[0] - section_index) % patch_total
    offset = jnp.sum(
        jnp.where(jnp.arange(patch_total, dtype=jnp.int32) == patch_number, patch_offsets, 0)
    )
    steps = jnp.array(STEPS, jnp.int32)
    outer = jnp.repeat(steps, SIDE)
    inner = jnp.tile(steps, SIDE)

    def chips_of(side, sign):
        down = jnp.where(side == 0, outer, inner)
        across = jnp.where(side == 0, inner, outer)
        return ((z + sign * down) % SIDE) * SIDE + (x + sign * across) % SIDE

    fresh_places = jnp.concatenate(
        [chips_of(core, -1) * 2 + core, chips_of(1 - core, -1) * 2 + (1 - core)]
    )
    patch_rows = kv_cache.shape[2] // patch_total
    spots = [
        jnp.concatenate([text_count[b : b + 1], fresh_places, (offset // patch_rows)[None]]).astype(
            jnp.int32
        )
        for b in range(2)
    ]
    sources = chips_of(core, 1)
    order = jnp.argsort(sources).astype(jnp.int32)

    entering = patch_in[0]
    mod_rows = modulation[0]
    weight = qkv_weight[0].T
    other_weight = swapped(weight)
    gain_q = jnp.pad(qk_gain[0, 0:1], ((0, 0), (0, HD)), constant_values=1.0)
    gain_k = jnp.pad(qk_gain[0, 1:2], ((0, 0), (0, HD)), constant_values=1.0)
    gains = jnp.concatenate([gain_q, gain_k], axis=0)

    normed = normed_rows(entering, mod_rows)

    def project(pieces):
        return projected_rows(pieces, weight, other_weight, gains)

    def joined_heads(near, far):
        own_q, own_kv, other_q, other_kv = (
            jnp.concatenate([a, b], axis=0) for a, b in zip(near, far, strict=True)
        )
        return own_q, own_kv, swapped(other_q), swapped(other_kv)

    def attend(emit, branch, q, kv_own, kv_other):
        return attended_rows(
            emit, spots[branch], branch, q, kv_cache[0], kv_own, kv_other, text_kv[0]
        )

    line = gather_first(normed[0])
    left, right = gather_second(line)
    far = gather_third(left, right)
    near_parts = project([line, left, right])
    second_rows = after(normed[1], left)
    line_1 = gather_first(second_rows)
    far_parts = project(list(far))
    q_own, kv_own, q_other, kv_other = joined_heads(near_parts, far_parts)
    left_1, right_1 = gather_second(line_1)
    away, fresh_0 = attend(True, 0, q_other, kv_own, kv_other)
    left_1, right_1, q_own = lax.optimization_barrier((left_1, right_1, after(q_own, away)))
    far_1 = gather_third(left_1, right_1)
    home_other = swapped(away)
    (home,) = attend(False, 0, q_own, kv_own, kv_other)

    near_parts = project([line_1, left_1, right_1])
    far_parts = project(list(far_1))
    q_own, kv_own, q_other, kv_other = joined_heads(near_parts, far_parts)

    def by_head(mine, other):
        first = jnp.where(core == 0, mine, other)
        second = jnp.where(core == 0, other, mine)
        return first, second

    blocks_0 = returned(*by_head(home, home_other))
    away_1, fresh_1 = attend(True, 1, q_other, kv_own, kv_other)
    done_0 = finished_rows(order, blocks_0, out_weight[0], entering, 0, mod_rows)
    section_pairs = [(i, (i + 1) % 4) for i in range(lax.axis_size("section"))]
    moved_0 = lax.ppermute(done_0, "section", section_pairs)
    home_other_1 = swapped(away_1)
    (home_1,) = attend(False, 1, q_own, kv_own, kv_other)
    blocks_1 = returned(*by_head(home_1, home_other_1))
    done_1 = finished_rows(order, blocks_1, out_weight[0], entering, 1, mod_rows)
    moved_1 = lax.ppermute(done_1, "section", section_pairs)
    moved = jnp.stack([moved_0, moved_1])
    return (moved[None], jnp.stack([fresh_0, fresh_1])[None])


def solution(mesh):
    in_specs = (
        P("section", None, "seq", None),
        P("section", None, None),
        P("section", None, "seq"),
        P("section", None, None),
        P("section", None, None),
        P("section", None, None, "seq"),
        P("section", None, None, "seq"),
        P(),
        P(),
        P(),
    )
    out_specs = (P("section", None, "seq", None), P("section", None, None, "seq"))
    return jax.shard_map(local, mesh=mesh, in_specs=in_specs, out_specs=out_specs, check_vma=False)
```

```python
import functools
import math

import jax
import jax.numpy as jnp
from jax import lax
from jax.experimental import pallas as pl
from jax.experimental.pallas import tpu as pltpu
from jax.sharding import PartitionSpec as P

HD = 64
SIDE = 4
CHIPS = SIDE * SIDE
STEPS = (0, 1, -1, 2)
MIB = 2**20


def pairs_of(phase, step):
    pairs = []
    for z in range(SIDE):
        for x in range(SIDE):
            for core in range(2):
                if (phase + core) % 2 == 0:
                    to = (z * SIDE + (x + step) % SIDE) * 2 + core
                else:
                    to = (((z + step) % SIDE) * SIDE + x) * 2 + core
                pairs.append(((z * SIDE + x) * 2 + core, to))
    return pairs


def along(value, phase, step):
    return lax.ppermute(value, "seq", pairs_of(phase, step))


def swapped(value):
    return lax.ppermute(value, "seq", [(i, i ^ 1) for i in range(2 * CHIPS)])


def after(value, *others):
    return lax.optimization_barrier((value, *others))[0]


def norm_kernel(x_ref, mod_ref, out_ref):
    shift = mod_ref[0:1, :]
    scale = 1.0 + mod_ref[1:2, :]
    rows = x_ref.shape[1]
    for branch in range(2):
        values = x_ref[branch].astype(jnp.float32)
        center = jnp.mean(values, axis=-1, keepdims=True)
        moved = values - center
        spread = jnp.mean(moved * moved, axis=-1, keepdims=True)
        out_ref[branch * rows : (branch + 1) * rows, :] = (
            moved * lax.rsqrt(spread + 1e-06) * scale + shift
        ).astype(jnp.bfloat16)


def normed_rows(entering, mod_rows):
    rows, width = entering.shape[1:]
    return pl.pallas_call(
        norm_kernel,
        out_shape=jax.ShapeDtypeStruct((2 * rows, width), jnp.bfloat16),
        compiler_params=pltpu.CompilerParams(vmem_limit_bytes=16 * MIB),
    )(entering, mod_rows)


def pack_kernel(own, other, out_ref):
    for at, weight in ((0, own), (4 * HD, other)):
        out_ref[at : at + 2 * HD, :] = weight[HD:, :]
        out_ref[at + 2 * HD : at + 3 * HD, :] = weight[:HD, :]
        out_ref[at + 3 * HD : at + 4 * HD, :] = jnp.zeros((HD, out_ref.shape[1]), out_ref.dtype)


def packed_rows(own, other):
    return pl.pallas_call(
        pack_kernel,
        out_shape=jax.ShapeDtypeStruct((8 * HD, own.shape[1]), own.dtype),
        compiler_params=pltpu.CompilerParams(vmem_limit_bytes=16 * MIB),
    )(own, other)


def split_kernel(*refs):
    parts, outs = refs[:-2], refs[-2:]
    rows = parts[0].shape[0] // 2
    for branch, out_ref in enumerate(outs):
        for i, part in enumerate(parts):
            out_ref[i * rows : (i + 1) * rows, :] = part[branch * rows : (branch + 1) * rows, :]


def split_rows(parts):
    rows, width = parts[0].shape
    out = jax.ShapeDtypeStruct((rows // 2 * len(parts), width), parts[0].dtype)
    return pl.pallas_call(
        split_kernel,
        out_shape=(out, out),
        compiler_params=pltpu.CompilerParams(vmem_limit_bytes=24 * MIB),
    )(*parts)


def project_kernel(*refs):
    pieces = refs[:-4]
    weight, gains, own_ref, other_ref = refs[-4:]
    lane = lax.broadcasted_iota(jnp.int32, (1, 2 * HD), 1)
    query_gain = gains[0:1, :]
    key_gain = gains[1:2, :]
    row = 0
    for piece in pieces:
        rows = piece.shape[0]
        for part, out_ref in ((0, own_ref), (4 * HD, other_ref)):
            out = lax.dot_general(
                piece[...],
                weight[part : part + 4 * HD, :],
                (((1,), (1,)), ((), ())),
                preferred_element_type=jnp.float32,
            )
            kv = out[:, : 2 * HD]
            q = out[:, 2 * HD :]
            key_square = jnp.where(lane < HD, kv * kv, 0.0)
            key_mean = jnp.sum(key_square, axis=-1, keepdims=True) * (1.0 / HD)
            key_scaled = kv * lax.rsqrt(key_mean + 1e-06) * key_gain
            out_ref[row : row + rows, : 2 * HD] = jnp.where(lane < HD, key_scaled, kv).astype(
                jnp.bfloat16
            )
            query_mean = jnp.sum(q * q, axis=-1, keepdims=True) * (1.0 / HD)
            out_ref[row : row + rows, 2 * HD :] = (
                q * lax.rsqrt(query_mean + 1e-06) * query_gain
            ).astype(jnp.bfloat16)
        row += rows


def projected_rows(pieces, packed_weight, gains):
    rows = sum(piece.shape[0] for piece in pieces)
    width = packed_weight.shape[1]
    out = jax.ShapeDtypeStruct((rows, 4 * HD), jnp.bfloat16)
    return pl.pallas_call(
        project_kernel,
        out_shape=(out, out),
        compiler_params=pltpu.CompilerParams(vmem_limit_bytes=40 * MIB),
        cost_estimate=pl.CostEstimate(
            flops=2 * rows * width * 512, bytes_accessed=rows * width * 2, transcendentals=0
        ),
    )(*pieces, packed_weight, gains)


def widened(kv, lane, last):
    wide = kv.astype(jnp.float32)
    front = jnp.where(lane < HD, wide, pltpu.roll(wide, HD, 1)).astype(jnp.bfloat16)
    back = jnp.where(lane < HD, wide, last).astype(jnp.bfloat16)
    pick = jnp.where(lax.broadcasted_iota(jnp.int32, (2 * HD, 2 * HD), 0) < HD, 1.0, 0.0)
    lengths = jnp.dot(
        (wide * wide).astype(jnp.bfloat16),
        pick.astype(jnp.bfloat16),
        preferred_element_type=jnp.float32,
    )
    return front, back, jnp.max(lengths, axis=0, keepdims=True)


def prepare_kernel(spots, first, second, third, text, kaug_ref, kv_ref, longest_ref):
    lane = lax.broadcasted_iota(jnp.int32, (1, 2 * HD), 1)
    start = 0
    longest = jnp.zeros((1, 2 * HD), jnp.float32)
    for source in (first, second, third, text):
        many = source.shape[0]
        kv = source[...]
        last = jnp.where((lane >= HD) & (lane < HD + 3), 1.0, 0.0)
        if source is text:
            used = lax.broadcasted_iota(jnp.int32, (many, 2 * HD), 0) < spots[pl.program_id(0)]
            last = jnp.where((lane == HD + 3) & jnp.logical_not(used), -30000.0, last)
        front, back, length = widened(kv, lane, last)
        kv_ref[start : start + many, :] = kv
        kaug_ref[start : start + many, : 2 * HD] = front
        kaug_ref[start : start + many, 2 * HD :] = back
        longest = jnp.maximum(longest, length)
        start += many
    longest_ref[...] = longest


def prepared_keys(spots, cache, text):
    branches = cache.shape[0]
    patch = cache.shape[1] // 4
    rows = 3 * patch + text.shape[1]

    def stale(step):
        return pl.BlockSpec(
            (None, patch, 2 * HD),
            lambda i, spots: (i, lax.rem(spots[2 + 2 * CHIPS] + step, 4), 0),
        )

    def each(*shape):
        return pl.BlockSpec((None, *shape), lambda i, spots: (i, 0, 0))

    return pl.pallas_call(
        prepare_kernel,
        out_shape=(
            jax.ShapeDtypeStruct((branches, rows, 4 * HD), jnp.bfloat16),
            jax.ShapeDtypeStruct((branches, rows, 2 * HD), jnp.bfloat16),
            jax.ShapeDtypeStruct((branches, 1, 2 * HD), jnp.float32),
        ),
        grid_spec=pltpu.PrefetchScalarGridSpec(
            num_scalar_prefetch=1,
            grid=(branches,),
            in_specs=[stale(1), stale(2), stale(3), each(text.shape[1], 2 * HD)],
            out_specs=(each(rows, 4 * HD), each(rows, 2 * HD), each(1, 2 * HD)),
        ),
        compiler_params=pltpu.CompilerParams(vmem_limit_bytes=40 * MIB),
        cost_estimate=pl.CostEstimate(
            flops=4 * rows * 128 * 128, bytes_accessed=rows * 2048, transcendentals=0
        ),
    )(spots, cache, cache, cache, text)


def attend_kernel(counts, branch, spots, *refs):
    pieces = refs[: sum(counts)]
    own_pieces, other_pieces = pieces[: counts[0]], pieces[counts[0] :]
    stale_kaug, stale_kv, stale_longest = refs[sum(counts) : sum(counts) + 3]
    out_ref, fresh_ref, kaug, kv_all, qaug, e_scr, total_ref, longest_ref, sems = refs[-9:]
    rows = qaug.shape[0]
    keys = kv_all.shape[0]
    stale = stale_kv.shape[1]
    lane = lax.broadcasted_iota(jnp.int32, (1, 2 * HD), 1)

    chunks = ((0, 2 * rows), (2 * rows, stale // 2), (2 * rows + stale // 2, stale // 2))
    wide_copy = pltpu.make_async_copy(stale_kaug.at[branch], kaug.at[pl.ds(2 * rows, stale), :], sems.at[0])
    kv_copy = pltpu.make_async_copy(stale_kv.at[branch], kv_all.at[pl.ds(2 * rows, stale), :], sems.at[1])

    @pl.when(pl.program_id(0) == 0)
    def _():
        wide_copy.start()
        kv_copy.start()
        start = 0
        longest = stale_longest[...]
        last = jnp.where((lane >= HD) & (lane < HD + 3), 1.0, 0.0)
        block = 0
        for source in pieces:
            many = source.shape[0]
            kv = source[:, : 2 * HD]
            front, back, length = widened(kv, lane, last)
            kv_all[start : start + many, :] = kv
            kaug[start : start + many, : 2 * HD] = front
            kaug[start : start + many, 2 * HD :] = back
            longest = jnp.maximum(longest, length)
            start += many
            for at in range(0, many, HD):
                to = pl.multiple_of(spots[2 + block] * HD, HD)
                fresh_ref[pl.ds(to, HD), :] = kv[at : at + HD, :]
                block += 1
        longest_ref[...] = longest

    own = pl.program_id(0) == 0
    scale = math.log2(math.e) / math.sqrt(HD)
    at = 0
    for mine, other in zip(own_pieces, other_pieces, strict=True):
        many = mine.shape[0]
        q = jnp.where(own, mine[:, 2 * HD :], other[:, 2 * HD :])
        scaled = q.astype(jnp.float32) * scale
        high = scaled.astype(jnp.bfloat16).astype(jnp.float32)
        left = scaled - high
        middle = left.astype(jnp.bfloat16).astype(jnp.float32)
        qaug[at : at + many, : 2 * HD] = (high + pltpu.roll(middle, HD, 1)).astype(jnp.bfloat16)
        qaug[at : at + many, 2 * HD :] = (left - middle).astype(jnp.bfloat16)
        total_ref[at : at + many, :] = jnp.broadcast_to(
            jnp.sum(scaled * scaled, axis=-1, keepdims=True), (many, 2 * HD)
        )
        at += many

    def lower(bound):
        one = bound.astype(jnp.bfloat16).astype(jnp.float32)
        rest = bound - one
        two = rest.astype(jnp.bfloat16).astype(jnp.float32)
        tail = jnp.where(lane == HD, -one, 1.0)
        tail = jnp.where(lane == HD + 1, -two, tail)
        tail = jnp.where(lane == HD + 2, two - rest, tail)
        tail = jnp.where(lane > HD + 3, 0.0, tail)
        low = qaug[:, 2 * HD :].astype(jnp.float32)
        qaug[:, 2 * HD :] = jnp.where(lane < HD, low, tail).astype(jnp.bfloat16)

    def scores(at, many):
        return lax.dot_general(
            qaug[...],
            kaug[at : at + many, :],
            (((1,), (1,)), ((), ())),
            preferred_element_type=jnp.float32,
        )

    def raise_chunk(at, many, total):
        raised = jnp.exp2(scores(at, many))
        e_scr[:, at : at + many] = raised
        for part in range(many // 128):
            total = total + raised[:, part * 128 : (part + 1) * 128]
        return total

    def keep_total(total):
        total_ref[...] = jnp.broadcast_to(jnp.sum(total, axis=-1, keepdims=True), (rows, 128))

    lower(jnp.sqrt(total_ref[...] * (longest_ref[...] * 1.02)) + 1e-3)
    total = raise_chunk(*chunks[0], jnp.zeros((rows, 128), jnp.float32))

    @pl.when(pl.program_id(0) == 0)
    def _():
        wide_copy.wait()
        kv_copy.wait()

    for chunk in chunks[1:]:
        total = raise_chunk(*chunk, total)
    keep_total(total)

    @pl.when(jnp.min(total_ref[...]) < 1e-12)
    def _():
        lower(jnp.zeros((rows, 2 * HD), jnp.float32))
        step = 2 * HD

        def best_of(j, best):
            at = pl.multiple_of(j * step, step)
            found = lax.dot_general(
                qaug[...],
                kaug[pl.ds(at, step), :],
                (((1,), (1,)), ((), ())),
                preferred_element_type=jnp.float32,
            )
            return jnp.maximum(best, found)

        best = lax.fori_loop(
            0, keys // step, best_of, jnp.full((rows, step), -3e38, jnp.float32)
        )
        best = jnp.max(best, axis=-1, keepdims=True)
        lower(jnp.broadcast_to(best, (rows, 2 * HD)))

        def raise_part(j, total):
            at = pl.multiple_of(j * step, step)
            raised = jnp.exp2(
                lax.dot_general(
                    qaug[...],
                    kaug[pl.ds(at, step), :],
                    (((1,), (1,)), ((), ())),
                    preferred_element_type=jnp.float32,
                )
            )
            e_scr[:, pl.ds(at, step)] = raised
            return total + raised

        keep_total(
            lax.fori_loop(0, keys // step, raise_part, jnp.zeros((rows, step), jnp.float32))
        )

    share = 1.0 / total_ref[...]
    def weigh(j, sums):
        at = pl.multiple_of(j * 2816, 2816)
        probs = e_scr[:, pl.ds(at, 2816)] * jnp.tile(share, (1, 2816 // 128))
        return sums + jnp.dot(
            probs.astype(jnp.bfloat16),
            kv_all[pl.ds(at, 2816), :],
            preferred_element_type=jnp.float32,
        )

    sums = lax.fori_loop(0, keys // 2816, weigh, jnp.zeros((rows, 2 * HD), jnp.float32))
    for block in range(CHIPS):
        top = sums[block * HD : block * HD + HD // 2, :]
        bottom = sums[block * HD + HD // 2 : (block + 1) * HD, :]
        joined = jnp.where(lane < HD, pltpu.roll(top, HD, 1), bottom)
        out_ref[spots[2 + pl.program_id(0) * CHIPS + block]] = joined.astype(jnp.bfloat16)


def attended_rows(spots, branch, own_pieces, other_pieces, prepared, earlier):
    pieces = (*own_pieces, *other_pieces)
    rows = sum(piece.shape[0] for piece in own_pieces)
    patch = 2 * rows
    keys = prepared[1].shape[1] + patch

    def whole(part):
        return pl.BlockSpec(part.shape, lambda i, spots: (0, 0))

    out_shape = (
        jax.ShapeDtypeStruct((2 * CHIPS, HD, 2 * HD), jnp.bfloat16),
        jax.ShapeDtypeStruct((2, patch, 2 * HD), jnp.bfloat16),
    )
    out_specs = (
        pl.BlockSpec((2 * CHIPS, HD // 2, 2 * HD), lambda i, spots: (0, branch, 0)),
        pl.BlockSpec((None, patch, 2 * HD), lambda i, spots: (branch, 0, 0)),
    )
    anywhere = pl.BlockSpec(memory_space=pl.ANY)
    return pl.pallas_call(
        functools.partial(attend_kernel, (len(own_pieces), len(other_pieces)), branch),
        out_shape=out_shape,
        grid_spec=pltpu.PrefetchScalarGridSpec(
            num_scalar_prefetch=1,
            grid=(2,),
            in_specs=[whole(part) for part in pieces]
            + [anywhere, anywhere]
            + [pl.BlockSpec((None, 1, 2 * HD), lambda i, spots: (branch, 0, 0))]
            + [anywhere] * len(earlier),
            out_specs=out_specs,
            scratch_shapes=[
                pltpu.VMEM((keys, 4 * HD), jnp.bfloat16),
                pltpu.VMEM((keys, 2 * HD), jnp.bfloat16),
                pltpu.VMEM((rows, 4 * HD), jnp.bfloat16),
                pltpu.VMEM((rows, keys), jnp.float32),
                pltpu.VMEM((rows, 2 * HD), jnp.float32),
                pltpu.VMEM((1, 2 * HD), jnp.float32),
                pltpu.SemaphoreType.DMA((2,)),
            ],
        ),
        input_output_aliases={1 + len(pieces) + 3 + i: i for i in range(len(earlier))},
        compiler_params=pltpu.CompilerParams(vmem_limit_bytes=48 * MIB),
        cost_estimate=pl.CostEstimate(
            flops=4 * patch * keys * 256, bytes_accessed=8 * MIB, transcendentals=0
        ),
    )(spots, *pieces, *prepared, *earlier)


def finish_kernel(heads, weight, entering, gate, out_ref, lhs, total):
    step = pl.program_id(0)
    rows = entering.shape[1]
    lane = lax.broadcasted_iota(jnp.int32, (1, 2 * HD), 1)

    @pl.when(step == 0)
    def _():
        for pair in range(CHIPS):
            low = heads[2 * pair].astype(jnp.float32)
            high = heads[2 * pair + 1].astype(jnp.float32)
            top = jnp.where(lane < HD, low, pltpu.roll(high, HD, 1)).astype(jnp.bfloat16)
            bottom = jnp.where(lane < HD, pltpu.roll(low, HD, 1), high).astype(jnp.bfloat16)
            at = (pair % SIDE) * 2 * HD
            for branch in range(2):
                from_row = branch * rows // 2
                to = branch * rows
                here = slice(at, at + 2 * HD)
                part = slice(from_row, from_row + rows // 2)
                lhs[pair // SIDE, to : to + rows // 2, here] = top[part]
                lhs[pair // SIDE, to + rows // 2 : to + rows, here] = bottom[part]

    part = jnp.dot(lhs[step], weight[...], preferred_element_type=jnp.float32)

    @pl.when(step == 0)
    def _():
        total[...] = part

    @pl.when(step > 0)
    def _():
        total[...] += part

    @pl.when(step == SIDE - 1)
    def _():
        for branch in range(2):
            sums = total[branch * rows : (branch + 1) * rows, :]
            out_ref[branch] = (entering[branch].astype(jnp.float32) + gate[2:3, :] * sums).astype(
                jnp.bfloat16
            )


def finished_rows(heads, weight, entering, mod_rows):
    rows, width = entering.shape[1:]
    depth = weight.shape[0] // SIDE
    return pl.pallas_call(
        finish_kernel,
        out_shape=jax.ShapeDtypeStruct(entering.shape, jnp.bfloat16),
        grid=(SIDE,),
        in_specs=[
            pl.BlockSpec(heads.shape, lambda i: (0, 0, 0)),
            pl.BlockSpec((depth, width), lambda i: (i, 0)),
            pl.BlockSpec(entering.shape, lambda i: (0, 0, 0)),
            pl.BlockSpec((3, width), lambda i: (0, 0)),
        ],
        out_specs=pl.BlockSpec(entering.shape, lambda i: (0, 0, 0)),
        scratch_shapes=[
            pltpu.VMEM((SIDE, 2 * rows, depth), jnp.bfloat16),
            pltpu.VMEM((2 * rows, width), jnp.float32),
        ],
        compiler_params=pltpu.CompilerParams(vmem_limit_bytes=24 * MIB),
        cost_estimate=pl.CostEstimate(
            flops=4 * rows * width * weight.shape[0],
            bytes_accessed=weight.shape[0] * width * 2,
            transcendentals=0,
        ),
    )(heads, weight, entering, mod_rows)


def local(
    patch_in,
    modulation,
    qkv_weight,
    qk_gain,
    out_weight,
    kv_cache,
    text_kv,
    patch_offsets,
    step_index,
    text_count,
):
    entering = patch_in[0]
    mod_rows = modulation[0]
    normed = normed_rows(entering, mod_rows)

    line = [normed] + [along(normed, 0, step) for step in STEPS[1:]]
    line_0, line_1 = split_rows(line)

    patch_offsets, step_index, text_count = after(
        (patch_offsets, step_index, text_count), normed
    )
    section_index = lax.axis_index("section")
    place = lax.axis_index("seq")
    core = place % 2
    x = (place // 2) % SIDE
    z = place // (2 * SIDE)
    patch_total = patch_offsets.shape[0]
    patch_number = (step_index[0] - section_index) % patch_total
    offset = jnp.sum(
        jnp.where(jnp.arange(patch_total, dtype=jnp.int32) == patch_number, patch_offsets, 0)
    )
    steps = jnp.array(STEPS, jnp.int32)
    outer = jnp.repeat(steps, SIDE)
    inner = jnp.tile(steps, SIDE)

    def chips_of(side):
        down = jnp.where(side == 0, outer, inner)
        across = jnp.where(side == 0, inner, outer)
        return ((z - down) % SIDE) * SIDE + (x - across) % SIDE

    fresh_places = jnp.concatenate(
        [chips_of(core) * 2 + core, chips_of(1 - core) * 2 + (1 - core)]
    )
    patch_rows = kv_cache.shape[2] // patch_total
    spots = jnp.concatenate([text_count, fresh_places, (offset // patch_rows)[None]])
    spots = spots.astype(jnp.int32)
    line_0, spots = lax.optimization_barrier((line_0, spots))
    left = along(line_0, 1, 1)
    right = along(line_0, 1, -1)
    cache, text, qkv_weight, qk_gain = after((kv_cache[0], text_kv[0], qkv_weight, qk_gain), line_0)
    weight = qkv_weight[0].T
    packed_weight = packed_rows(weight, swapped(weight))
    gains = jnp.pad(qk_gain[0], ((0, 0), (0, HD)), constant_values=1.0)
    prepared = prepared_keys(spots, cache, text)
    left, right, prepared, packed_weight, gains = lax.optimization_barrier(
        (left, right, prepared, packed_weight, gains)
    )

    def project(pieces):
        own, other = projected_rows(pieces, packed_weight, gains)
        return own, swapped(other)

    half = line_0.shape[0] // 2
    far_low = along(left[:half], 1, 1)
    far_high = along(right[half:], 1, -1)
    own_near, other_near = project([line_0, left, right])
    far_low, far_high, line_1 = lax.optimization_barrier((far_low, far_high, line_1))
    left_1 = along(line_1, 1, 1)
    right_1 = along(line_1, 1, -1)
    far_1 = along(line_1, 1, 2)
    own_far, other_far = project([far_low, far_high])
    first = attended_rows(
        spots, 0, (own_near, own_far), (other_near, other_far), prepared, ()
    )
    left_1, right_1, far_1, first = lax.optimization_barrier((left_1, right_1, far_1, first))
    own_all, other_all = project([line_1, left_1, right_1, far_1])
    attended, fresh = attended_rows(spots, 1, (own_all,), (other_all,), prepared, first)

    heads = lax.all_to_all(attended, "seq", split_axis=0, concat_axis=0, tiled=True)
    done = finished_rows(heads, out_weight[0], entering, mod_rows)
    count = lax.axis_size("section")
    moved = lax.ppermute(done, "section", [(i, (i + 1) % count) for i in range(count)])
    return (moved[None], fresh[None])


def solution(mesh):
    in_specs = (
        P("section", None, "seq", None),
        P("section", None, None),
        P("section", None, "seq"),
        P("section", None, None),
        P("section", None, None),
        P("section", None, None, "seq"),
        P("section", None, None, "seq"),
        P(),
        P(),
        P(),
    )
    out_specs = (P("section", None, "seq", None), P("section", None, None, "seq"))
    return jax.shard_map(local, mesh=mesh, in_specs=in_specs, out_specs=out_specs, check_vma=False)
```

```python
import functools
import math

import jax
import jax.numpy as jnp
from jax import lax
from jax.experimental import pallas as pl
from jax.experimental.pallas import tpu as pltpu
from jax.sharding import PartitionSpec as P

HD = 64
SIDE = 4
CHIPS = SIDE * SIDE
STEPS = (0, 1, -1, 2)
MIB = 2**20


def pairs_of(phase, step):
    pairs = []
    for z in range(SIDE):
        for x in range(SIDE):
            for core in range(2):
                if (phase + core) % 2 == 0:
                    to = (z * SIDE + (x + step) % SIDE) * 2 + core
                else:
                    to = (((z + step) % SIDE) * SIDE + x) * 2 + core
                pairs.append(((z * SIDE + x) * 2 + core, to))
    return pairs


def along(value, phase, step):
    return lax.ppermute(value, "seq", pairs_of(phase, step))


def swapped(value):
    return lax.ppermute(value, "seq", [(i, i ^ 1) for i in range(2 * CHIPS)])


def after(value, *others):
    return lax.optimization_barrier((value, *others))[0]


def norm_kernel(x_ref, mod_ref, out_ref):
    values = x_ref[...].astype(jnp.float32)
    center = jnp.mean(values, axis=-1, keepdims=True)
    moved = values - center
    spread = jnp.mean(moved * moved, axis=-1, keepdims=True)
    scaled = moved * lax.rsqrt(spread + 1e-06) * (1.0 + mod_ref[1:2, :])
    out_ref[...] = (scaled + mod_ref[0:1, :]).astype(jnp.bfloat16)


def normed_rows(entering, branch, mod_rows):
    rows, width = entering.shape[1:]
    return pl.pallas_call(
        norm_kernel,
        out_shape=jax.ShapeDtypeStruct((rows, width), jnp.bfloat16),
        grid=(1,),
        in_specs=[
            pl.BlockSpec((None, rows, width), lambda i: (branch, 0, 0)),
            pl.BlockSpec(mod_rows.shape, lambda i: (0, 0)),
        ],
        out_specs=pl.BlockSpec((rows, width), lambda i: (0, 0)),
        compiler_params=pltpu.CompilerParams(vmem_limit_bytes=16 * MIB),
    )(entering, mod_rows)


def pack_kernel(own, other, out_ref):
    for at, weight in ((0, own), (4 * HD, other)):
        out_ref[at : at + 2 * HD, :] = weight[HD:, :]
        out_ref[at + 2 * HD : at + 3 * HD, :] = weight[:HD, :]
        out_ref[at + 3 * HD : at + 4 * HD, :] = jnp.zeros((HD, out_ref.shape[1]), out_ref.dtype)


def packed_rows(own, other):
    return pl.pallas_call(
        pack_kernel,
        out_shape=jax.ShapeDtypeStruct((8 * HD, own.shape[1]), own.dtype),
        compiler_params=pltpu.CompilerParams(vmem_limit_bytes=16 * MIB),
    )(own, other)


def join_kernel(*refs):
    parts, outs = refs[:-2], refs[-2:]
    rows = parts[0].shape[0]
    for i, part in enumerate(parts):
        at = i % 2 * rows
        outs[i // 2][at : at + rows, :] = part[...]


def joined_rows(parts):
    rows, width = parts[0].shape
    out = jax.ShapeDtypeStruct((2 * rows, width), parts[0].dtype)
    return pl.pallas_call(
        join_kernel,
        out_shape=(out, out),
        compiler_params=pltpu.CompilerParams(vmem_limit_bytes=16 * MIB),
    )(*parts)


def project_kernel(*refs):
    pieces = refs[:-4]
    weight, gains, own_ref, other_ref = refs[-4:]
    lane = lax.broadcasted_iota(jnp.int32, (1, 2 * HD), 1)
    query_gain = gains[0:1, :]
    key_gain = gains[1:2, :]
    row = 0
    for piece in pieces:
        rows = piece.shape[0]
        for part, out_ref in ((0, own_ref), (4 * HD, other_ref)):
            out = lax.dot_general(
                piece[...],
                weight[part : part + 4 * HD, :],
                (((1,), (1,)), ((), ())),
                preferred_element_type=jnp.float32,
            )
            kv = out[:, : 2 * HD]
            q = out[:, 2 * HD :]
            key_square = jnp.where(lane < HD, kv * kv, 0.0)
            key_mean = jnp.sum(key_square, axis=-1, keepdims=True) * (1.0 / HD)
            key_scaled = kv * lax.rsqrt(key_mean + 1e-06) * key_gain
            out_ref[row : row + rows, : 2 * HD] = jnp.where(lane < HD, key_scaled, kv).astype(
                jnp.bfloat16
            )
            query_mean = jnp.sum(q * q, axis=-1, keepdims=True) * (1.0 / HD)
            out_ref[row : row + rows, 2 * HD :] = (
                q * lax.rsqrt(query_mean + 1e-06) * query_gain
            ).astype(jnp.bfloat16)
        row += rows


def projected_rows(pieces, packed_weight, gains):
    rows = sum(piece.shape[0] for piece in pieces)
    width = packed_weight.shape[1]
    out = jax.ShapeDtypeStruct((rows, 4 * HD), jnp.bfloat16)
    return pl.pallas_call(
        project_kernel,
        out_shape=(out, out),
        compiler_params=pltpu.CompilerParams(vmem_limit_bytes=40 * MIB),
        cost_estimate=pl.CostEstimate(
            flops=2 * rows * width * 512, bytes_accessed=rows * width * 2, transcendentals=0
        ),
    )(*pieces, packed_weight, gains)


def widened(kv, lane, last):
    wide = kv.astype(jnp.float32)
    front = jnp.where(lane < HD, wide, pltpu.roll(wide, HD, 1)).astype(jnp.bfloat16)
    back = jnp.where(lane < HD, wide, last).astype(jnp.bfloat16)
    pick = jnp.where(lax.broadcasted_iota(jnp.int32, (2 * HD, 2 * HD), 0) < HD, 1.0, 0.0)
    lengths = jnp.dot(
        (wide * wide).astype(jnp.bfloat16),
        pick.astype(jnp.bfloat16),
        preferred_element_type=jnp.float32,
    )
    return front, back, jnp.max(lengths, axis=0, keepdims=True)


def prepare_kernel(spots, first, second, third, text, kaug_ref, kv_ref, longest_ref):
    lane = lax.broadcasted_iota(jnp.int32, (1, 2 * HD), 1)
    start = 0
    longest = jnp.zeros((1, 2 * HD), jnp.float32)
    for source in (first, second, third, text):
        many = source.shape[0]
        kv = source[...]
        last = jnp.where((lane >= HD) & (lane < HD + 3), 1.0, 0.0)
        if source is text:
            used = lax.broadcasted_iota(jnp.int32, (many, 2 * HD), 0) < spots[pl.program_id(0)]
            last = jnp.where((lane == HD + 3) & jnp.logical_not(used), -30000.0, last)
        front, back, length = widened(kv, lane, last)
        kv_ref[start : start + many, :] = kv
        kaug_ref[start : start + many, : 2 * HD] = front
        kaug_ref[start : start + many, 2 * HD :] = back
        longest = jnp.maximum(longest, length)
        start += many
    longest_ref[...] = longest


def prepared_keys(spots, cache, text):
    branches = cache.shape[0]
    patch = cache.shape[1] // 4
    rows = 3 * patch + text.shape[1]

    def stale(step):
        return pl.BlockSpec(
            (None, patch, 2 * HD),
            lambda i, spots: (i, lax.rem(spots[2 + 2 * CHIPS] + step, 4), 0),
        )

    def each(*shape):
        return pl.BlockSpec((None, *shape), lambda i, spots: (i, 0, 0))

    return pl.pallas_call(
        prepare_kernel,
        out_shape=(
            jax.ShapeDtypeStruct((branches, rows, 4 * HD), jnp.bfloat16),
            jax.ShapeDtypeStruct((branches, rows, 2 * HD), jnp.bfloat16),
            jax.ShapeDtypeStruct((branches, 1, 2 * HD), jnp.float32),
        ),
        grid_spec=pltpu.PrefetchScalarGridSpec(
            num_scalar_prefetch=1,
            grid=(branches,),
            in_specs=[stale(1), stale(2), stale(3), each(text.shape[1], 2 * HD)],
            out_specs=(each(rows, 4 * HD), each(rows, 2 * HD), each(1, 2 * HD)),
        ),
        compiler_params=pltpu.CompilerParams(vmem_limit_bytes=60 * MIB),
        cost_estimate=pl.CostEstimate(
            flops=4 * rows * 128 * 128, bytes_accessed=rows * 2048, transcendentals=0
        ),
    )(spots, cache, cache, cache, text)


def attend_kernel(counts, branch, spots, *refs):
    pieces = refs[: sum(counts)]
    own_pieces, other_pieces = pieces[: counts[0]], pieces[counts[0] :]
    stale_kaug, stale_kv, stale_longest = refs[sum(counts) : sum(counts) + 3]
    out_ref, fresh_ref, kaug, kv_all, qaug, e_scr, total_ref, longest_ref, sems = refs[-9:]
    rows = qaug.shape[0]
    keys = kv_all.shape[0]
    stale = stale_kv.shape[1]
    lane = lax.broadcasted_iota(jnp.int32, (1, 2 * HD), 1)

    chunks = ((0, 2 * rows), (2 * rows, stale // 2), (2 * rows + stale // 2, stale // 2))
    wide_copy = pltpu.make_async_copy(stale_kaug.at[branch], kaug.at[pl.ds(2 * rows, stale), :], sems.at[0])
    kv_copy = pltpu.make_async_copy(stale_kv.at[branch], kv_all.at[pl.ds(2 * rows, stale), :], sems.at[1])

    @pl.when(pl.program_id(0) == 0)
    def _():
        wide_copy.start()
        kv_copy.start()
        start = 0
        longest = stale_longest[...]
        last = jnp.where((lane >= HD) & (lane < HD + 3), 1.0, 0.0)
        block = 0
        for source in pieces:
            many = source.shape[0]
            kv = source[:, : 2 * HD]
            front, back, length = widened(kv, lane, last)
            kv_all[start : start + many, :] = kv
            kaug[start : start + many, : 2 * HD] = front
            kaug[start : start + many, 2 * HD :] = back
            longest = jnp.maximum(longest, length)
            start += many
            for at in range(0, many, HD):
                to = pl.multiple_of(spots[2 + block] * HD, HD)
                fresh_ref[pl.ds(to, HD), :] = kv[at : at + HD, :]
                block += 1
        longest_ref[...] = longest

    own = pl.program_id(0) == 0
    scale = math.log2(math.e) / math.sqrt(HD)
    at = 0
    for mine, other in zip(own_pieces, other_pieces, strict=True):
        many = mine.shape[0]
        q = jnp.where(own, mine[:, 2 * HD :], other[:, 2 * HD :])
        scaled = q.astype(jnp.float32) * scale
        high = scaled.astype(jnp.bfloat16).astype(jnp.float32)
        left = scaled - high
        middle = left.astype(jnp.bfloat16).astype(jnp.float32)
        qaug[at : at + many, : 2 * HD] = (high + pltpu.roll(middle, HD, 1)).astype(jnp.bfloat16)
        qaug[at : at + many, 2 * HD :] = (left - middle).astype(jnp.bfloat16)
        total_ref[at : at + many, :] = jnp.broadcast_to(
            jnp.sum(scaled * scaled, axis=-1, keepdims=True), (many, 2 * HD)
        )
        at += many

    def lower(bound):
        one = bound.astype(jnp.bfloat16).astype(jnp.float32)
        rest = bound - one
        two = rest.astype(jnp.bfloat16).astype(jnp.float32)
        tail = jnp.where(lane == HD, -one, 1.0)
        tail = jnp.where(lane == HD + 1, -two, tail)
        tail = jnp.where(lane == HD + 2, two - rest, tail)
        tail = jnp.where(lane > HD + 3, 0.0, tail)
        low = qaug[:, 2 * HD :].astype(jnp.float32)
        qaug[:, 2 * HD :] = jnp.where(lane < HD, low, tail).astype(jnp.bfloat16)

    def scores(at, many):
        return lax.dot_general(
            qaug[...],
            kaug[at : at + many, :],
            (((1,), (1,)), ((), ())),
            preferred_element_type=jnp.float32,
        )

    def raise_chunk(at, many, total):
        raised = jnp.exp2(scores(at, many))
        e_scr[:, at : at + many] = raised
        for part in range(many // 128):
            total = total + raised[:, part * 128 : (part + 1) * 128]
        return total

    def keep_total(total):
        total_ref[...] = jnp.broadcast_to(jnp.sum(total, axis=-1, keepdims=True), (rows, 128))

    lower(jnp.sqrt(total_ref[...] * (longest_ref[...] * 1.02)) + 1e-3)
    total = raise_chunk(*chunks[0], jnp.zeros((rows, 128), jnp.float32))

    @pl.when(pl.program_id(0) == 0)
    def _():
        wide_copy.wait()
        kv_copy.wait()

    for chunk in chunks[1:]:
        total = raise_chunk(*chunk, total)
    keep_total(total)

    @pl.when(jnp.min(total_ref[...]) < 1e-12)
    def _():
        lower(jnp.zeros((rows, 2 * HD), jnp.float32))
        step = 2 * HD

        def best_of(j, best):
            at = pl.multiple_of(j * step, step)
            found = lax.dot_general(
                qaug[...],
                kaug[pl.ds(at, step), :],
                (((1,), (1,)), ((), ())),
                preferred_element_type=jnp.float32,
            )
            return jnp.maximum(best, found)

        best = lax.fori_loop(
            0, keys // step, best_of, jnp.full((rows, step), -3e38, jnp.float32)
        )
        best = jnp.max(best, axis=-1, keepdims=True)
        lower(jnp.broadcast_to(best, (rows, 2 * HD)))

        def raise_part(j, total):
            at = pl.multiple_of(j * step, step)
            raised = jnp.exp2(
                lax.dot_general(
                    qaug[...],
                    kaug[pl.ds(at, step), :],
                    (((1,), (1,)), ((), ())),
                    preferred_element_type=jnp.float32,
                )
            )
            e_scr[:, pl.ds(at, step)] = raised
            return total + raised

        keep_total(
            lax.fori_loop(0, keys // step, raise_part, jnp.zeros((rows, step), jnp.float32))
        )

    share = 1.0 / total_ref[...]
    def weigh(j, sums):
        at = pl.multiple_of(j * 2816, 2816)
        probs = e_scr[:, pl.ds(at, 2816)] * jnp.tile(share, (1, 2816 // 128))
        return sums + jnp.dot(
            probs.astype(jnp.bfloat16),
            kv_all[pl.ds(at, 2816), :],
            preferred_element_type=jnp.float32,
        )

    sums = lax.fori_loop(0, keys // 2816, weigh, jnp.zeros((rows, 2 * HD), jnp.float32))
    for block in range(CHIPS):
        top = sums[block * HD : block * HD + HD // 2, :]
        bottom = sums[block * HD + HD // 2 : (block + 1) * HD, :]
        joined = jnp.where(lane < HD, pltpu.roll(top, HD, 1), bottom)
        out_ref[spots[2 + pl.program_id(0) * CHIPS + block]] = joined.astype(jnp.bfloat16)


def attended_rows(spots, branch, own_pieces, other_pieces, prepared, earlier):
    pieces = (*own_pieces, *other_pieces)
    rows = sum(piece.shape[0] for piece in own_pieces)
    patch = 2 * rows
    keys = prepared[1].shape[1] + patch

    def whole(part):
        return pl.BlockSpec(part.shape, lambda i, spots: (0, 0))

    out_shape = (
        jax.ShapeDtypeStruct((2 * CHIPS, HD, 2 * HD), jnp.bfloat16),
        jax.ShapeDtypeStruct((2, patch, 2 * HD), jnp.bfloat16),
    )
    out_specs = (
        pl.BlockSpec((2 * CHIPS, HD // 2, 2 * HD), lambda i, spots: (0, branch, 0)),
        pl.BlockSpec((None, patch, 2 * HD), lambda i, spots: (branch, 0, 0)),
    )
    anywhere = pl.BlockSpec(memory_space=pl.ANY)
    return pl.pallas_call(
        functools.partial(attend_kernel, (len(own_pieces), len(other_pieces)), branch),
        out_shape=out_shape,
        grid_spec=pltpu.PrefetchScalarGridSpec(
            num_scalar_prefetch=1,
            grid=(2,),
            in_specs=[whole(part) for part in pieces]
            + [anywhere, anywhere]
            + [pl.BlockSpec((None, 1, 2 * HD), lambda i, spots: (branch, 0, 0))]
            + [anywhere] * len(earlier),
            out_specs=out_specs,
            scratch_shapes=[
                pltpu.VMEM((keys, 4 * HD), jnp.bfloat16),
                pltpu.VMEM((keys, 2 * HD), jnp.bfloat16),
                pltpu.VMEM((rows, 4 * HD), jnp.bfloat16),
                pltpu.VMEM((rows, keys), jnp.float32),
                pltpu.VMEM((rows, 2 * HD), jnp.float32),
                pltpu.VMEM((1, 2 * HD), jnp.float32),
                pltpu.SemaphoreType.DMA((2,)),
            ],
        ),
        input_output_aliases={1 + len(pieces) + 3 + i: i for i in range(len(earlier))},
        compiler_params=pltpu.CompilerParams(vmem_limit_bytes=48 * MIB),
        cost_estimate=pl.CostEstimate(
            flops=4 * patch * keys * 256, bytes_accessed=8 * MIB, transcendentals=0
        ),
    )(spots, *pieces, *prepared, *earlier)


def finish_kernel(heads, weight, entering, gate, out_ref, lhs, total):
    step = pl.program_id(0)
    rows = entering.shape[1]
    lane = lax.broadcasted_iota(jnp.int32, (1, 2 * HD), 1)

    @pl.when(step == 0)
    def _():
        for pair in range(CHIPS):
            low = heads[2 * pair].astype(jnp.float32)
            high = heads[2 * pair + 1].astype(jnp.float32)
            top = jnp.where(lane < HD, low, pltpu.roll(high, HD, 1)).astype(jnp.bfloat16)
            bottom = jnp.where(lane < HD, pltpu.roll(low, HD, 1), high).astype(jnp.bfloat16)
            at = (pair % SIDE) * 2 * HD
            for branch in range(2):
                from_row = branch * rows // 2
                to = branch * rows
                here = slice(at, at + 2 * HD)
                part = slice(from_row, from_row + rows // 2)
                lhs[pair // SIDE, to : to + rows // 2, here] = top[part]
                lhs[pair // SIDE, to + rows // 2 : to + rows, here] = bottom[part]

    part = jnp.dot(lhs[step], weight[...], preferred_element_type=jnp.float32)

    @pl.when(step == 0)
    def _():
        total[...] = part

    @pl.when(step > 0)
    def _():
        total[...] += part

    @pl.when(step == SIDE - 1)
    def _():
        for branch in range(2):
            sums = total[branch * rows : (branch + 1) * rows, :]
            out_ref[branch] = (entering[branch].astype(jnp.float32) + gate[2:3, :] * sums).astype(
                jnp.bfloat16
            )


def finished_rows(heads, weight, entering, mod_rows):
    rows, width = entering.shape[1:]
    depth = weight.shape[0] // SIDE
    return pl.pallas_call(
        finish_kernel,
        out_shape=jax.ShapeDtypeStruct(entering.shape, jnp.bfloat16),
        grid=(SIDE,),
        in_specs=[
            pl.BlockSpec(heads.shape, lambda i: (0, 0, 0)),
            pl.BlockSpec((depth, width), lambda i: (i, 0)),
            pl.BlockSpec(entering.shape, lambda i: (0, 0, 0)),
            pl.BlockSpec((3, width), lambda i: (0, 0)),
        ],
        out_specs=pl.BlockSpec(entering.shape, lambda i: (0, 0, 0)),
        scratch_shapes=[
            pltpu.VMEM((SIDE, 2 * rows, depth), jnp.bfloat16),
            pltpu.VMEM((2 * rows, width), jnp.float32),
        ],
        compiler_params=pltpu.CompilerParams(vmem_limit_bytes=24 * MIB),
        cost_estimate=pl.CostEstimate(
            flops=4 * rows * width * weight.shape[0],
            bytes_accessed=weight.shape[0] * width * 2,
            transcendentals=0,
        ),
    )(heads, weight, entering, mod_rows)


def local(
    patch_in,
    modulation,
    qkv_weight,
    qk_gain,
    out_weight,
    kv_cache,
    text_kv,
    patch_offsets,
    step_index,
    text_count,
):
    entering = patch_in[0]
    mod_rows = modulation[0]
    def first_round(rows):
        return [rows] + [along(rows, 0, step) for step in STEPS[1:]]

    line = first_round(normed_rows(entering, 0, mod_rows))

    patch_offsets, step_index, text_count = after(
        (patch_offsets, step_index, text_count), line[0]
    )
    section_index = lax.axis_index("section")
    place = lax.axis_index("seq")
    core = place % 2
    x = (place // 2) % SIDE
    z = place // (2 * SIDE)
    patch_total = patch_offsets.shape[0]
    patch_number = (step_index[0] - section_index) % patch_total
    offset = jnp.sum(
        jnp.where(jnp.arange(patch_total, dtype=jnp.int32) == patch_number, patch_offsets, 0)
    )
    steps = jnp.array(STEPS, jnp.int32)
    outer = jnp.repeat(steps, SIDE)
    inner = jnp.tile(steps, SIDE)

    def chips_of(side):
        down = jnp.where(side == 0, outer, inner)
        across = jnp.where(side == 0, inner, outer)
        return ((z - down) % SIDE) * SIDE + (x - across) % SIDE

    fresh_places = jnp.concatenate(
        [chips_of(core) * 2 + core, chips_of(1 - core) * 2 + (1 - core)]
    )
    patch_rows = kv_cache.shape[2] // patch_total
    spots = jnp.concatenate([text_count, fresh_places, (offset // patch_rows)[None]])
    spots = spots.astype(jnp.int32)
    line_1 = first_round(normed_rows(after(entering, offset), 1, mod_rows))
    low, high = joined_rows(line)
    low, high, spots = lax.optimization_barrier((low, high, spots))
    left_low = along(low, 1, 1)
    right_high = along(high, 1, -1)
    left_high = along(high, 1, 1)
    right_low = along(low, 1, -1)
    cache, text, qkv_weight, qk_gain = after((kv_cache[0], text_kv[0], qkv_weight, qk_gain), low)
    weight = qkv_weight[0].T
    packed_weight = packed_rows(weight, swapped(weight))
    gains = jnp.pad(qk_gain[0], ((0, 0), (0, HD)), constant_values=1.0)
    prepared = prepared_keys(spots, cache, text)
    left_low, right_high, prepared, packed_weight, gains = lax.optimization_barrier(
        (left_low, right_high, prepared, packed_weight, gains)
    )

    def project(pieces):
        own, other = projected_rows(pieces, packed_weight, gains)
        return own, swapped(other)

    far_low = along(left_low, 1, 1)
    far_high = along(right_high, 1, -1)
    own_near, other_near = project([low, high, left_low, left_high, right_low, right_high])
    line_1 = after(jnp.concatenate(line_1, axis=0), far_low, far_high)
    left_1 = along(line_1, 1, 1)
    right_1 = along(line_1, 1, -1)
    far_1 = along(line_1, 1, 2)
    own_far, other_far = project([far_low, far_high])
    first = attended_rows(
        spots, 0, (own_near, own_far), (other_near, other_far), prepared, ()
    )
    left_1, right_1, far_1, first = lax.optimization_barrier((left_1, right_1, far_1, first))
    own_all, other_all = project([line_1, left_1, right_1, far_1])
    attended, fresh = attended_rows(spots, 1, (own_all,), (other_all,), prepared, first)

    heads = lax.all_to_all(attended, "seq", split_axis=0, concat_axis=0, tiled=True)
    done = finished_rows(heads, out_weight[0], entering, mod_rows)
    count = lax.axis_size("section")
    moved = lax.ppermute(done, "section", [(i, (i + 1) % count) for i in range(count)])
    return (moved[None], fresh[None])


def solution(mesh):
    in_specs = (
        P("section", None, "seq", None),
        P("section", None, None),
        P("section", None, "seq"),
        P("section", None, None),
        P("section", None, None),
        P("section", None, None, "seq"),
        P("section", None, None, "seq"),
        P(),
        P(),
        P(),
    )
    out_specs = (P("section", None, "seq", None), P("section", None, None, "seq"))
    return jax.shard_map(local, mesh=mesh, in_specs=in_specs, out_specs=out_specs, check_vma=False)
```

```python
import functools
import math

import jax
import jax.numpy as jnp
from jax import lax
from jax.experimental import pallas as pl
from jax.experimental.pallas import tpu as pltpu
from jax.sharding import PartitionSpec as P

HD = 64
SIDE = 4
CHIPS = SIDE * SIDE
STEPS = (0, 1, -1, 2)
MIB = 2**20


def pairs_of(phase, step):
    pairs = []
    for z in range(SIDE):
        for x in range(SIDE):
            for core in range(2):
                if (phase + core) % 2 == 0:
                    to = (z * SIDE + (x + step) % SIDE) * 2 + core
                else:
                    to = (((z + step) % SIDE) * SIDE + x) * 2 + core
                pairs.append(((z * SIDE + x) * 2 + core, to))
    return pairs


def along(value, phase, step):
    return lax.ppermute(value, "seq", pairs_of(phase, step))


def swapped(value):
    return lax.ppermute(value, "seq", [(i, i ^ 1) for i in range(2 * CHIPS)])


def after(value, *others):
    return lax.optimization_barrier((value, *others))[0]


def norm_kernel(x_ref, mod_ref, out_ref):
    values = x_ref[...].astype(jnp.float32)
    center = jnp.mean(values, axis=-1, keepdims=True)
    moved = values - center
    spread = jnp.mean(moved * moved, axis=-1, keepdims=True)
    scaled = moved * lax.rsqrt(spread + 1e-06) * (1.0 + mod_ref[1:2, :])
    out_ref[...] = (scaled + mod_ref[0:1, :]).astype(jnp.bfloat16)


def normed_rows(entering, branch, mod_rows):
    rows, width = entering.shape[1:]
    return pl.pallas_call(
        norm_kernel,
        out_shape=jax.ShapeDtypeStruct((rows, width), jnp.bfloat16),
        grid=(1,),
        in_specs=[
            pl.BlockSpec((None, rows, width), lambda i: (branch, 0, 0)),
            pl.BlockSpec(mod_rows.shape, lambda i: (0, 0)),
        ],
        out_specs=pl.BlockSpec((rows, width), lambda i: (0, 0)),
        compiler_params=pltpu.CompilerParams(vmem_limit_bytes=16 * MIB),
    )(entering, mod_rows)


def pack_kernel(own, other, out_ref):
    for at, weight in ((0, own), (4 * HD, other)):
        out_ref[at : at + 2 * HD, :] = weight[HD:, :]
        out_ref[at + 2 * HD : at + 3 * HD, :] = weight[:HD, :]
        out_ref[at + 3 * HD : at + 4 * HD, :] = jnp.zeros((HD, out_ref.shape[1]), out_ref.dtype)


def packed_rows(own, other):
    return pl.pallas_call(
        pack_kernel,
        out_shape=jax.ShapeDtypeStruct((8 * HD, own.shape[1]), own.dtype),
        compiler_params=pltpu.CompilerParams(vmem_limit_bytes=16 * MIB),
    )(own, other)


def join_kernel(*refs):
    parts, outs = refs[:-2], refs[-2:]
    rows = parts[0].shape[0]
    for i, part in enumerate(parts):
        at = i % 2 * rows
        outs[i // 2][at : at + rows, :] = part[...]


def joined_rows(parts):
    rows, width = parts[0].shape
    out = jax.ShapeDtypeStruct((2 * rows, width), parts[0].dtype)
    return pl.pallas_call(
        join_kernel,
        out_shape=(out, out),
        compiler_params=pltpu.CompilerParams(vmem_limit_bytes=16 * MIB),
    )(*parts)


def project_kernel(count, *refs):
    pieces = refs[:count]
    weight, gains, own_ref, other_ref, joined = refs[count:]
    lane = lax.broadcasted_iota(jnp.int32, (1, 2 * HD), 1)
    query_gain = gains[0:1, :]
    key_gain = gains[1:2, :]

    def block(rows, here):
        for part, out_ref in ((0, own_ref), (4 * HD, other_ref)):
            out = lax.dot_general(
                rows,
                weight[part : part + 4 * HD, :],
                (((1,), (1,)), ((), ())),
                preferred_element_type=jnp.float32,
            )
            kv = out[:, : 2 * HD]
            q = out[:, 2 * HD :]
            key_square = jnp.where(lane < HD, kv * kv, 0.0)
            key_mean = jnp.sum(key_square, axis=-1, keepdims=True) * (1.0 / HD)
            key_scaled = kv * lax.rsqrt(key_mean + 1e-06) * key_gain
            out_ref[here, : 2 * HD] = jnp.where(lane < HD, key_scaled, kv).astype(jnp.bfloat16)
            query_mean = jnp.sum(q * q, axis=-1, keepdims=True) * (1.0 / HD)
            out_ref[here, 2 * HD :] = (q * lax.rsqrt(query_mean + 1e-06) * query_gain).astype(
                jnp.bfloat16
            )

    row = 0
    if pieces[0].shape[0] == joined.shape[0]:
        for piece in pieces:
            block(piece[...], slice(row, row + piece.shape[0]))
            row += piece.shape[0]
        return

    step = 4 * HD
    for piece in pieces:
        joined[row : row + piece.shape[0], :] = piece[...]
        row += piece.shape[0]

    @pl.loop(0, row // step)
    def _(i):
        here = pl.ds(pl.multiple_of(i * step, step), step)
        block(joined[here, :], here)


def projected_rows(pieces, packed_weight, gains):
    rows = sum(piece.shape[0] for piece in pieces)
    width = packed_weight.shape[1]
    out = jax.ShapeDtypeStruct((rows, 4 * HD), jnp.bfloat16)
    large = pieces[0].shape[0] == 4 * HD
    return pl.pallas_call(
        functools.partial(project_kernel, len(pieces)),
        out_shape=(out, out),
        scratch_shapes=[pltpu.VMEM((4 * HD if large else rows, width), jnp.bfloat16)],
        compiler_params=pltpu.CompilerParams(vmem_limit_bytes=40 * MIB),
        cost_estimate=pl.CostEstimate(
            flops=2 * rows * width * 512, bytes_accessed=rows * width * 2, transcendentals=0
        ),
    )(*pieces, packed_weight, gains)


def widened(kv, lane, last):
    wide = kv.astype(jnp.float32)
    front = jnp.where(lane < HD, wide, pltpu.roll(wide, HD, 1)).astype(jnp.bfloat16)
    back = jnp.where(lane < HD, wide, last).astype(jnp.bfloat16)
    pick = jnp.where(lax.broadcasted_iota(jnp.int32, (2 * HD, 2 * HD), 0) < HD, 1.0, 0.0)
    lengths = jnp.dot(
        (wide * wide).astype(jnp.bfloat16),
        pick.astype(jnp.bfloat16),
        preferred_element_type=jnp.float32,
    )
    return front, back, jnp.max(lengths, axis=0, keepdims=True)


def prepare_kernel(spots, first, second, third, text, kaug_ref, kv_ref, longest_ref):
    lane = lax.broadcasted_iota(jnp.int32, (1, 2 * HD), 1)
    start = 0
    longest = jnp.zeros((1, 2 * HD), jnp.float32)
    for source in (first, second, third, text):
        many = source.shape[0]
        kv = source[...]
        last = jnp.where((lane >= HD) & (lane < HD + 3), 1.0, 0.0)
        if source is text:
            used = lax.broadcasted_iota(jnp.int32, (many, 2 * HD), 0) < spots[pl.program_id(0)]
            last = jnp.where((lane == HD + 3) & jnp.logical_not(used), -30000.0, last)
        front, back, length = widened(kv, lane, last)
        kv_ref[start : start + many, :] = kv
        kaug_ref[start : start + many, : 2 * HD] = front
        kaug_ref[start : start + many, 2 * HD :] = back
        longest = jnp.maximum(longest, length)
        start += many
    longest_ref[...] = longest


def prepared_keys(spots, cache, text):
    branches = cache.shape[0]
    patch = cache.shape[1] // 4
    rows = 3 * patch + text.shape[1]

    def stale(step):
        return pl.BlockSpec(
            (None, patch, 2 * HD),
            lambda i, spots: (i, lax.rem(spots[2 + 2 * CHIPS] + step, 4), 0),
        )

    def each(*shape):
        return pl.BlockSpec((None, *shape), lambda i, spots: (i, 0, 0))

    return pl.pallas_call(
        prepare_kernel,
        out_shape=(
            jax.ShapeDtypeStruct((branches, rows, 4 * HD), jnp.bfloat16),
            jax.ShapeDtypeStruct((branches, rows, 2 * HD), jnp.bfloat16),
            jax.ShapeDtypeStruct((branches, 1, 2 * HD), jnp.float32),
        ),
        grid_spec=pltpu.PrefetchScalarGridSpec(
            num_scalar_prefetch=1,
            grid=(branches,),
            in_specs=[stale(1), stale(2), stale(3), each(text.shape[1], 2 * HD)],
            out_specs=(each(rows, 4 * HD), each(rows, 2 * HD), each(1, 2 * HD)),
        ),
        compiler_params=pltpu.CompilerParams(vmem_limit_bytes=60 * MIB),
        cost_estimate=pl.CostEstimate(
            flops=4 * rows * 128 * 128, bytes_accessed=rows * 2048, transcendentals=0
        ),
    )(spots, cache, cache, cache, text)


def attend_kernel(counts, branch, spots, *refs):
    pieces = refs[: sum(counts)]
    own_pieces, other_pieces = pieces[: counts[0]], pieces[counts[0] :]
    stale_kaug, stale_kv, stale_longest = refs[sum(counts) : sum(counts) + 3]
    out_ref, fresh_ref, kaug, kv_all, qaug, e_scr, total_ref, longest_ref, sems = refs[-9:]
    rows = qaug.shape[0]
    keys = kv_all.shape[0]
    stale = stale_kv.shape[1]
    lane = lax.broadcasted_iota(jnp.int32, (1, 2 * HD), 1)

    chunks = ((0, 2 * rows), (2 * rows, stale // 2), (2 * rows + stale // 2, stale // 2))
    wide_copy = pltpu.make_async_copy(stale_kaug.at[branch], kaug.at[pl.ds(2 * rows, stale), :], sems.at[0])
    kv_copy = pltpu.make_async_copy(stale_kv.at[branch], kv_all.at[pl.ds(2 * rows, stale), :], sems.at[1])

    @pl.when(pl.program_id(0) == 0)
    def _():
        wide_copy.start()
        kv_copy.start()
        start = 0
        longest = stale_longest[...]
        last = jnp.where((lane >= HD) & (lane < HD + 3), 1.0, 0.0)
        block = 0
        for source in pieces:
            many = source.shape[0]
            kv = source[:, : 2 * HD]
            front, back, length = widened(kv, lane, last)
            kv_all[start : start + many, :] = kv
            kaug[start : start + many, : 2 * HD] = front
            kaug[start : start + many, 2 * HD :] = back
            longest = jnp.maximum(longest, length)
            start += many
            for at in range(0, many, HD):
                to = pl.multiple_of(spots[2 + block] * HD, HD)
                fresh_ref[pl.ds(to, HD), :] = kv[at : at + HD, :]
                block += 1
        longest_ref[...] = longest

    own = pl.program_id(0) == 0
    scale = math.log2(math.e) / math.sqrt(HD)
    at = 0
    for mine, other in zip(own_pieces, other_pieces, strict=True):
        many = mine.shape[0]
        q = jnp.where(own, mine[:, 2 * HD :], other[:, 2 * HD :])
        scaled = q.astype(jnp.float32) * scale
        high = scaled.astype(jnp.bfloat16).astype(jnp.float32)
        left = scaled - high
        middle = left.astype(jnp.bfloat16).astype(jnp.float32)
        qaug[at : at + many, : 2 * HD] = (high + pltpu.roll(middle, HD, 1)).astype(jnp.bfloat16)
        qaug[at : at + many, 2 * HD :] = (left - middle).astype(jnp.bfloat16)
        total_ref[at : at + many, :] = jnp.broadcast_to(
            jnp.sum(scaled * scaled, axis=-1, keepdims=True), (many, 2 * HD)
        )
        at += many

    def lower(bound):
        one = bound.astype(jnp.bfloat16).astype(jnp.float32)
        rest = bound - one
        two = rest.astype(jnp.bfloat16).astype(jnp.float32)
        tail = jnp.where(lane == HD, -one, 1.0)
        tail = jnp.where(lane == HD + 1, -two, tail)
        tail = jnp.where(lane == HD + 2, two - rest, tail)
        tail = jnp.where(lane > HD + 3, 0.0, tail)
        low = qaug[:, 2 * HD :].astype(jnp.float32)
        qaug[:, 2 * HD :] = jnp.where(lane < HD, low, tail).astype(jnp.bfloat16)

    def scores(at, many):
        return lax.dot_general(
            qaug[...],
            kaug[at : at + many, :],
            (((1,), (1,)), ((), ())),
            preferred_element_type=jnp.float32,
        )

    def raise_chunk(at, many, total):
        raised = jnp.exp2(scores(at, many))
        e_scr[:, at : at + many] = raised
        for part in range(many // 128):
            total = total + raised[:, part * 128 : (part + 1) * 128]
        return total

    def keep_total(total):
        total_ref[...] = jnp.broadcast_to(jnp.sum(total, axis=-1, keepdims=True), (rows, 128))

    lower(jnp.sqrt(total_ref[...] * (longest_ref[...] * 1.02)) + 1e-3)
    total = raise_chunk(*chunks[0], jnp.zeros((rows, 128), jnp.float32))

    @pl.when(pl.program_id(0) == 0)
    def _():
        wide_copy.wait()
        kv_copy.wait()

    for chunk in chunks[1:]:
        total = raise_chunk(*chunk, total)
    keep_total(total)

    @pl.when(jnp.min(total_ref[...]) < 1e-12)
    def _():
        lower(jnp.zeros((rows, 2 * HD), jnp.float32))
        step = 2 * HD

        def best_of(j, best):
            at = pl.multiple_of(j * step, step)
            found = lax.dot_general(
                qaug[...],
                kaug[pl.ds(at, step), :],
                (((1,), (1,)), ((), ())),
                preferred_element_type=jnp.float32,
            )
            return jnp.maximum(best, found)

        best = lax.fori_loop(
            0, keys // step, best_of, jnp.full((rows, step), -3e38, jnp.float32)
        )
        best = jnp.max(best, axis=-1, keepdims=True)
        lower(jnp.broadcast_to(best, (rows, 2 * HD)))

        def raise_part(j, total):
            at = pl.multiple_of(j * step, step)
            raised = jnp.exp2(
                lax.dot_general(
                    qaug[...],
                    kaug[pl.ds(at, step), :],
                    (((1,), (1,)), ((), ())),
                    preferred_element_type=jnp.float32,
                )
            )
            e_scr[:, pl.ds(at, step)] = raised
            return total + raised

        keep_total(
            lax.fori_loop(0, keys // step, raise_part, jnp.zeros((rows, step), jnp.float32))
        )

    share = 1.0 / total_ref[...]
    def weigh(j, sums):
        at = pl.multiple_of(j * 2816, 2816)
        probs = e_scr[:, pl.ds(at, 2816)] * jnp.tile(share, (1, 2816 // 128))
        return sums + jnp.dot(
            probs.astype(jnp.bfloat16),
            kv_all[pl.ds(at, 2816), :],
            preferred_element_type=jnp.float32,
        )

    sums = lax.fori_loop(0, keys // 2816, weigh, jnp.zeros((rows, 2 * HD), jnp.float32))
    for block in range(CHIPS):
        top = sums[block * HD : block * HD + HD // 2, :]
        bottom = sums[block * HD + HD // 2 : (block + 1) * HD, :]
        joined = jnp.where(lane < HD, pltpu.roll(top, HD, 1), bottom)
        out_ref[spots[2 + pl.program_id(0) * CHIPS + block]] = joined.astype(jnp.bfloat16)


def attended_rows(spots, branch, own_pieces, other_pieces, prepared, earlier):
    pieces = (*own_pieces, *other_pieces)
    rows = sum(piece.shape[0] for piece in own_pieces)
    patch = 2 * rows
    keys = prepared[1].shape[1] + patch

    def whole(part):
        return pl.BlockSpec(part.shape, lambda i, spots: (0, 0))

    out_shape = (
        jax.ShapeDtypeStruct((2 * CHIPS, HD, 2 * HD), jnp.bfloat16),
        jax.ShapeDtypeStruct((2, patch, 2 * HD), jnp.bfloat16),
    )
    out_specs = (
        pl.BlockSpec((2 * CHIPS, HD // 2, 2 * HD), lambda i, spots: (0, branch, 0)),
        pl.BlockSpec((None, patch, 2 * HD), lambda i, spots: (branch, 0, 0)),
    )
    anywhere = pl.BlockSpec(memory_space=pl.ANY)
    return pl.pallas_call(
        functools.partial(attend_kernel, (len(own_pieces), len(other_pieces)), branch),
        out_shape=out_shape,
        grid_spec=pltpu.PrefetchScalarGridSpec(
            num_scalar_prefetch=1,
            grid=(2,),
            in_specs=[whole(part) for part in pieces]
            + [anywhere, anywhere]
            + [pl.BlockSpec((None, 1, 2 * HD), lambda i, spots: (branch, 0, 0))]
            + [anywhere] * len(earlier),
            out_specs=out_specs,
            scratch_shapes=[
                pltpu.VMEM((keys, 4 * HD), jnp.bfloat16),
                pltpu.VMEM((keys, 2 * HD), jnp.bfloat16),
                pltpu.VMEM((rows, 4 * HD), jnp.bfloat16),
                pltpu.VMEM((rows, keys), jnp.float32),
                pltpu.VMEM((rows, 2 * HD), jnp.float32),
                pltpu.VMEM((1, 2 * HD), jnp.float32),
                pltpu.SemaphoreType.DMA((2,)),
            ],
        ),
        input_output_aliases={1 + len(pieces) + 3 + i: i for i in range(len(earlier))},
        compiler_params=pltpu.CompilerParams(vmem_limit_bytes=48 * MIB),
        cost_estimate=pl.CostEstimate(
            flops=4 * patch * keys * 256, bytes_accessed=8 * MIB, transcendentals=0
        ),
    )(spots, *pieces, *prepared, *earlier)


def finish_kernel(columns, heads, weight, entering, gate, out_ref, lhs):
    rows = entering.shape[1]
    lane = lax.broadcasted_iota(jnp.int32, (1, 2 * HD), 1)
    for pair in range(CHIPS):
        low = heads[2 * pair].astype(jnp.float32)
        high = heads[2 * pair + 1].astype(jnp.float32)
        top = jnp.where(lane < HD, low, pltpu.roll(high, HD, 1)).astype(jnp.bfloat16)
        bottom = jnp.where(lane < HD, pltpu.roll(low, HD, 1), high).astype(jnp.bfloat16)
        here = slice(pair * 2 * HD, (pair + 1) * 2 * HD)
        for branch in range(2):
            to = branch * rows
            part = slice(branch * rows // 2, (branch + 1) * rows // 2)
            lhs[to : to + rows // 2, here] = top[part]
            lhs[to + rows // 2 : to + rows, here] = bottom[part]
    sums = jnp.dot(lhs[...], weight[:, columns], preferred_element_type=jnp.float32)
    for branch in range(2):
        part = sums[branch * rows : (branch + 1) * rows]
        out_ref[branch] = (
            entering[branch, :, columns].astype(jnp.float32) + gate[2:3, columns] * part
        ).astype(jnp.bfloat16)


def finished_rows(heads, weight, entering, mod_rows, columns):
    branches, rows = entering.shape[:2]
    width = columns.stop - columns.start
    return pl.pallas_call(
        functools.partial(finish_kernel, columns),
        out_shape=jax.ShapeDtypeStruct((branches, rows, width), jnp.bfloat16),
        scratch_shapes=[pltpu.VMEM((branches * rows, weight.shape[0]), jnp.bfloat16)],
        compiler_params=pltpu.CompilerParams(vmem_limit_bytes=24 * MIB),
        cost_estimate=pl.CostEstimate(
            flops=4 * rows * width * weight.shape[0],
            bytes_accessed=weight.shape[0] * width * 2,
            transcendentals=0,
        ),
    )(heads, weight, entering, mod_rows)


def local(
    patch_in,
    modulation,
    qkv_weight,
    qk_gain,
    out_weight,
    kv_cache,
    text_kv,
    patch_offsets,
    step_index,
    text_count,
):
    entering = patch_in[0]
    mod_rows = modulation[0]
    def first_round(rows):
        return [rows] + [along(rows, 0, step) for step in STEPS[1:]]

    line = first_round(normed_rows(entering, 0, mod_rows))

    patch_offsets, step_index, text_count = after(
        (patch_offsets, step_index, text_count), line[0]
    )
    section_index = lax.axis_index("section")
    place = lax.axis_index("seq")
    core = place % 2
    x = (place // 2) % SIDE
    z = place // (2 * SIDE)
    patch_total = patch_offsets.shape[0]
    patch_number = (step_index[0] - section_index) % patch_total
    offset = jnp.sum(
        jnp.where(jnp.arange(patch_total, dtype=jnp.int32) == patch_number, patch_offsets, 0)
    )
    steps = jnp.array(STEPS, jnp.int32)
    outer = jnp.repeat(steps, SIDE)
    inner = jnp.tile(steps, SIDE)

    def chips_of(side):
        down = jnp.where(side == 0, outer, inner)
        across = jnp.where(side == 0, inner, outer)
        return ((z - down) % SIDE) * SIDE + (x - across) % SIDE

    fresh_places = jnp.concatenate(
        [chips_of(core) * 2 + core, chips_of(1 - core) * 2 + (1 - core)]
    )
    patch_rows = kv_cache.shape[2] // patch_total
    spots = jnp.concatenate([text_count, fresh_places, (offset // patch_rows)[None]])
    spots = spots.astype(jnp.int32)
    line_1 = first_round(normed_rows(after(entering, offset), 1, mod_rows))
    low, high = joined_rows(line)
    low, high, spots = lax.optimization_barrier((low, high, spots))
    left_low = along(low, 1, 1)
    right_high = along(high, 1, -1)
    left_high = along(high, 1, 1)
    right_low = along(low, 1, -1)
    cache, text, qkv_weight, qk_gain = after((kv_cache[0], text_kv[0], qkv_weight, qk_gain), low)
    weight = qkv_weight[0].T
    packed_weight = packed_rows(weight, swapped(weight))
    gains = jnp.pad(qk_gain[0], ((0, 0), (0, HD)), constant_values=1.0)
    prepared = prepared_keys(spots, cache, text)
    left_low, right_high, prepared, packed_weight, gains = lax.optimization_barrier(
        (left_low, right_high, prepared, packed_weight, gains)
    )

    def project(pieces):
        own, other = projected_rows(pieces, packed_weight, gains)
        return own, swapped(other)

    far_low = along(left_low, 1, 1)
    far_high = along(right_high, 1, -1)
    own_near, other_near = project([low, high, left_low, left_high, right_low, right_high])
    line_1 = after(jnp.concatenate(line_1, axis=0), far_low, far_high)
    left_1 = along(line_1, 1, 1)
    right_1 = along(line_1, 1, -1)
    far_1 = along(line_1, 1, 2)
    own_far, other_far = project([far_low, far_high])
    first = attended_rows(
        spots, 0, (own_near, own_far), (other_near, other_far), prepared, ()
    )
    left_1, right_1, far_1, first = lax.optimization_barrier((left_1, right_1, far_1, first))
    own_all, other_all = project([line_1, left_1, right_1, far_1])
    attended, fresh = attended_rows(spots, 1, (own_all,), (other_all,), prepared, first)

    heads = lax.all_to_all(attended, "seq", split_axis=0, concat_axis=0, tiled=True)
    count = lax.axis_size("section")
    width = entering.shape[2]
    cut = width // 256 * 128 + 128
    moved = []
    for columns in (slice(0, cut), slice(cut, width)):
        done = finished_rows(heads, out_weight[0], entering, mod_rows, columns)
        moved.append(lax.ppermute(done, "section", [(i, (i + 1) % count) for i in range(count)]))
    moved = jnp.concatenate(moved, axis=-1)
    return (moved[None], fresh[None])


def solution(mesh):
    in_specs = (
        P("section", None, "seq", None),
        P("section", None, None),
        P("section", None, "seq"),
        P("section", None, None),
        P("section", None, None),
        P("section", None, None, "seq"),
        P("section", None, None, "seq"),
        P(),
        P(),
        P(),
    )
    out_specs = (P("section", None, "seq", None), P("section", None, None, "seq"))
    return jax.shard_map(local, mesh=mesh, in_specs=in_specs, out_specs=out_specs, check_vma=False)
```

```python
import functools
import math

import jax
import jax.numpy as jnp
from jax import lax
from jax.experimental import pallas as pl
from jax.experimental.pallas import tpu as pltpu
from jax.sharding import PartitionSpec as P

HD = 64
SIDE = 4
CHIPS = SIDE * SIDE
STEPS = (0, 1, -1, 2)
MIB = 2**20


def pairs_of(phase, step):
    pairs = []
    for z in range(SIDE):
        for x in range(SIDE):
            for core in range(2):
                if (phase + core) % 2 == 0:
                    to = (z * SIDE + (x + step) % SIDE) * 2 + core
                else:
                    to = (((z + step) % SIDE) * SIDE + x) * 2 + core
                pairs.append(((z * SIDE + x) * 2 + core, to))
    return pairs


def along(value, phase, step):
    return lax.ppermute(value, "seq", pairs_of(phase, step))


def swapped(value):
    return lax.ppermute(value, "seq", [(i, i ^ 1) for i in range(2 * CHIPS)])


def after(value, *others):
    return lax.optimization_barrier((value, *others))[0]


def norm_kernel(x_ref, mod_ref, out_ref):
    values = x_ref[...].astype(jnp.float32)
    center = jnp.mean(values, axis=-1, keepdims=True)
    moved = values - center
    spread = jnp.mean(moved * moved, axis=-1, keepdims=True)
    scaled = moved * lax.rsqrt(spread + 1e-06) * (1.0 + mod_ref[1:2, :])
    out_ref[...] = (scaled + mod_ref[0:1, :]).astype(jnp.bfloat16)


def normed_rows(entering, branch, mod_rows):
    rows, width = entering.shape[1:]
    return pl.pallas_call(
        norm_kernel,
        out_shape=jax.ShapeDtypeStruct((rows, width), jnp.bfloat16),
        grid=(1,),
        in_specs=[
            pl.BlockSpec((None, rows, width), lambda i: (branch, 0, 0)),
            pl.BlockSpec(mod_rows.shape, lambda i: (0, 0)),
        ],
        out_specs=pl.BlockSpec((rows, width), lambda i: (0, 0)),
        compiler_params=pltpu.CompilerParams(vmem_limit_bytes=16 * MIB),
    )(entering, mod_rows)


def pack_kernel(own, other, out_ref):
    for at, weight in ((0, own), (4 * HD, other)):
        out_ref[at : at + 2 * HD, :] = weight[HD:, :]
        out_ref[at + 2 * HD : at + 3 * HD, :] = weight[:HD, :]
        out_ref[at + 3 * HD : at + 4 * HD, :] = jnp.zeros((HD, out_ref.shape[1]), out_ref.dtype)


def packed_rows(own, other):
    return pl.pallas_call(
        pack_kernel,
        out_shape=jax.ShapeDtypeStruct((8 * HD, own.shape[1]), own.dtype),
        compiler_params=pltpu.CompilerParams(vmem_limit_bytes=16 * MIB),
    )(own, other)


def join_kernel(*refs):
    parts, outs = refs[:-2], refs[-2:]
    rows = parts[0].shape[0]
    for i, part in enumerate(parts):
        at = i % 2 * rows
        outs[i // 2][at : at + rows, :] = part[...]


def joined_rows(parts):
    rows, width = parts[0].shape
    out = jax.ShapeDtypeStruct((2 * rows, width), parts[0].dtype)
    return pl.pallas_call(
        join_kernel,
        out_shape=(out, out),
        compiler_params=pltpu.CompilerParams(vmem_limit_bytes=16 * MIB),
    )(*parts)


def project_kernel(count, *refs):
    pieces = refs[:count]
    weight, gains, own_ref, other_ref, joined = refs[count:]
    lane = lax.broadcasted_iota(jnp.int32, (1, 2 * HD), 1)
    query_gain = gains[0:1, :]
    key_gain = gains[1:2, :]

    def block(rows, here):
        for part, out_ref in ((0, own_ref), (4 * HD, other_ref)):
            out = lax.dot_general(
                rows,
                weight[part : part + 4 * HD, :],
                (((1,), (1,)), ((), ())),
                preferred_element_type=jnp.float32,
            )
            kv = out[:, : 2 * HD]
            q = out[:, 2 * HD :]
            key_square = jnp.where(lane < HD, kv * kv, 0.0)
            key_mean = jnp.sum(key_square, axis=-1, keepdims=True) * (1.0 / HD)
            key_scaled = kv * lax.rsqrt(key_mean + 1e-06) * key_gain
            out_ref[here, : 2 * HD] = jnp.where(lane < HD, key_scaled, kv).astype(jnp.bfloat16)
            query_mean = jnp.sum(q * q, axis=-1, keepdims=True) * (1.0 / HD)
            out_ref[here, 2 * HD :] = (q * lax.rsqrt(query_mean + 1e-06) * query_gain).astype(
                jnp.bfloat16
            )

    row = 0
    if pieces[0].shape[0] == joined.shape[0]:
        for piece in pieces:
            block(piece[...], slice(row, row + piece.shape[0]))
            row += piece.shape[0]
        return

    step = 4 * HD
    for piece in pieces:
        joined[row : row + piece.shape[0], :] = piece[...]
        row += piece.shape[0]

    @pl.loop(0, row // step)
    def _(i):
        here = pl.ds(pl.multiple_of(i * step, step), step)
        block(joined[here, :], here)


def projected_rows(pieces, packed_weight, gains):
    rows = sum(piece.shape[0] for piece in pieces)
    width = packed_weight.shape[1]
    out = jax.ShapeDtypeStruct((rows, 4 * HD), jnp.bfloat16)
    large = pieces[0].shape[0] == 4 * HD
    return pl.pallas_call(
        functools.partial(project_kernel, len(pieces)),
        out_shape=(out, out),
        scratch_shapes=[pltpu.VMEM((4 * HD if large else rows, width), jnp.bfloat16)],
        compiler_params=pltpu.CompilerParams(vmem_limit_bytes=40 * MIB),
        cost_estimate=pl.CostEstimate(
            flops=2 * rows * width * 512, bytes_accessed=rows * width * 2, transcendentals=0
        ),
    )(*pieces, packed_weight, gains)


def widened(kv, lane, last):
    wide = kv.astype(jnp.float32)
    front = jnp.where(lane < HD, wide, pltpu.roll(wide, HD, 1)).astype(jnp.bfloat16)
    back = jnp.where(lane < HD, wide, last).astype(jnp.bfloat16)
    pick = jnp.where(lax.broadcasted_iota(jnp.int32, (2 * HD, 2 * HD), 0) < HD, 1.0, 0.0)
    lengths = jnp.dot(
        (wide * wide).astype(jnp.bfloat16),
        pick.astype(jnp.bfloat16),
        preferred_element_type=jnp.float32,
    )
    return front, back, jnp.max(lengths, axis=0, keepdims=True)


def prepare_kernel(spots, first, second, third, text, kaug_ref, longest_ref):
    lane = lax.broadcasted_iota(jnp.int32, (1, 2 * HD), 1)
    start = 0
    longest = jnp.zeros((1, 2 * HD), jnp.float32)
    for source in (first, second, third, text):
        many = source.shape[0]
        kv = source[...]
        last = jnp.where((lane >= HD) & (lane < HD + 3), 1.0, 0.0)
        if source is text:
            used = lax.broadcasted_iota(jnp.int32, (many, 2 * HD), 0) < spots[pl.program_id(0)]
            last = jnp.where((lane == HD + 3) & jnp.logical_not(used), -30000.0, last)
        front, back, length = widened(kv, lane, last)
        kaug_ref[start : start + many, : 2 * HD] = front
        kaug_ref[start : start + many, 2 * HD :] = back
        longest = jnp.maximum(longest, length)
        start += many
    longest_ref[...] = longest


def prepared_keys(spots, cache, text):
    branches = cache.shape[0]
    patch = cache.shape[1] // 4
    rows = 3 * patch + text.shape[1]

    def stale(step):
        return pl.BlockSpec(
            (None, patch, 2 * HD),
            lambda i, spots: (i, lax.rem(spots[2 + 2 * CHIPS] + step, 4), 0),
        )

    def each(*shape):
        return pl.BlockSpec((None, *shape), lambda i, spots: (i, 0, 0))

    return pl.pallas_call(
        prepare_kernel,
        out_shape=(
            jax.ShapeDtypeStruct((branches, rows, 4 * HD), jnp.bfloat16),
            jax.ShapeDtypeStruct((branches, 1, 2 * HD), jnp.float32),
        ),
        grid_spec=pltpu.PrefetchScalarGridSpec(
            num_scalar_prefetch=1,
            grid=(branches,),
            in_specs=[stale(1), stale(2), stale(3), each(text.shape[1], 2 * HD)],
            out_specs=(each(rows, 4 * HD), each(1, 2 * HD)),
        ),
        compiler_params=pltpu.CompilerParams(vmem_limit_bytes=60 * MIB),
        cost_estimate=pl.CostEstimate(
            flops=4 * rows * 128 * 128, bytes_accessed=rows * 2048, transcendentals=0
        ),
    )(spots, cache, cache, cache, text)


def attend_kernel(counts, branch, spots, *refs):
    pieces = refs[: sum(counts)]
    own_pieces, other_pieces = pieces[: counts[0]], pieces[counts[0] :]
    stale_kaug, stale_longest, cache, text = refs[sum(counts) : sum(counts) + 4]
    out_ref, fresh_ref, kaug, kv_all, qaug, e_scr, total_ref, longest_ref, sems = refs[-9:]
    rows = qaug.shape[0]
    keys = kv_all.shape[0]
    stale = stale_kaug.shape[1]
    lane = lax.broadcasted_iota(jnp.int32, (1, 2 * HD), 1)

    chunks = ((0, 2 * rows), (2 * rows, stale // 2), (2 * rows + stale // 2, stale // 2))
    wide_copy = pltpu.make_async_copy(stale_kaug.at[branch], kaug.at[pl.ds(2 * rows, stale), :], sems.at[0])
    patch = 2 * rows
    copies = [wide_copy]
    for i in range(1, 4):
        at = lax.rem(spots[2 + 2 * CHIPS] + i, 4) * patch
        copies.append(
            pltpu.make_async_copy(
                cache.at[branch, pl.ds(pl.multiple_of(at, patch), patch), :],
                kv_all.at[pl.ds(i * patch, patch), :],
                sems.at[i],
            )
        )
    copies.append(
        pltpu.make_async_copy(
            text.at[branch], kv_all.at[pl.ds(4 * patch, keys - 4 * patch), :], sems.at[4]
        )
    )

    @pl.when(pl.program_id(0) == 0)
    def _():
        for copy in copies:
            copy.start()
        start = 0
        longest = stale_longest[...]
        last = jnp.where((lane >= HD) & (lane < HD + 3), 1.0, 0.0)
        block = 0
        for source in pieces:
            many = source.shape[0]
            kv = source[:, : 2 * HD]
            front, back, length = widened(kv, lane, last)
            kv_all[start : start + many, :] = kv
            kaug[start : start + many, : 2 * HD] = front
            kaug[start : start + many, 2 * HD :] = back
            longest = jnp.maximum(longest, length)
            start += many
            for at in range(0, many, HD):
                to = pl.multiple_of(spots[2 + block] * HD, HD)
                fresh_ref[pl.ds(to, HD), :] = kv[at : at + HD, :]
                block += 1
        longest_ref[...] = longest

    own = pl.program_id(0) == 0
    scale = math.log2(math.e) / math.sqrt(HD)
    at = 0
    for mine, other in zip(own_pieces, other_pieces, strict=True):
        many = mine.shape[0]
        q = jnp.where(own, mine[:, 2 * HD :], other[:, 2 * HD :])
        scaled = q.astype(jnp.float32) * scale
        high = scaled.astype(jnp.bfloat16).astype(jnp.float32)
        left = scaled - high
        middle = left.astype(jnp.bfloat16).astype(jnp.float32)
        qaug[at : at + many, : 2 * HD] = (high + pltpu.roll(middle, HD, 1)).astype(jnp.bfloat16)
        qaug[at : at + many, 2 * HD :] = (left - middle).astype(jnp.bfloat16)
        total_ref[at : at + many, :] = jnp.broadcast_to(
            jnp.sum(scaled * scaled, axis=-1, keepdims=True), (many, 2 * HD)
        )
        at += many

    def lower(bound):
        one = bound.astype(jnp.bfloat16).astype(jnp.float32)
        rest = bound - one
        two = rest.astype(jnp.bfloat16).astype(jnp.float32)
        tail = jnp.where(lane == HD, -one, 1.0)
        tail = jnp.where(lane == HD + 1, -two, tail)
        tail = jnp.where(lane == HD + 2, two - rest, tail)
        tail = jnp.where(lane > HD + 3, 0.0, tail)
        low = qaug[:, 2 * HD :].astype(jnp.float32)
        qaug[:, 2 * HD :] = jnp.where(lane < HD, low, tail).astype(jnp.bfloat16)

    def scores(at, many):
        return lax.dot_general(
            qaug[...],
            kaug[at : at + many, :],
            (((1,), (1,)), ((), ())),
            preferred_element_type=jnp.float32,
        )

    def raise_chunk(at, many, total):
        raised = jnp.exp2(scores(at, many))
        e_scr[:, at : at + many] = raised
        for part in range(many // 128):
            total = total + raised[:, part * 128 : (part + 1) * 128]
        return total

    def keep_total(total):
        total_ref[...] = jnp.broadcast_to(jnp.sum(total, axis=-1, keepdims=True), (rows, 128))

    lower(jnp.sqrt(total_ref[...] * (longest_ref[...] * 1.02)) + 1e-3)
    total = raise_chunk(*chunks[0], jnp.zeros((rows, 128), jnp.float32))

    @pl.when(pl.program_id(0) == 0)
    def _():
        for copy in copies:
            copy.wait()

    for chunk in chunks[1:]:
        total = raise_chunk(*chunk, total)
    keep_total(total)

    @pl.when(jnp.min(total_ref[...]) < 1e-12)
    def _():
        lower(jnp.zeros((rows, 2 * HD), jnp.float32))
        step = 2 * HD

        def best_of(j, best):
            at = pl.multiple_of(j * step, step)
            found = lax.dot_general(
                qaug[...],
                kaug[pl.ds(at, step), :],
                (((1,), (1,)), ((), ())),
                preferred_element_type=jnp.float32,
            )
            return jnp.maximum(best, found)

        best = lax.fori_loop(
            0, keys // step, best_of, jnp.full((rows, step), -3e38, jnp.float32)
        )
        best = jnp.max(best, axis=-1, keepdims=True)
        lower(jnp.broadcast_to(best, (rows, 2 * HD)))

        def raise_part(j, total):
            at = pl.multiple_of(j * step, step)
            raised = jnp.exp2(
                lax.dot_general(
                    qaug[...],
                    kaug[pl.ds(at, step), :],
                    (((1,), (1,)), ((), ())),
                    preferred_element_type=jnp.float32,
                )
            )
            e_scr[:, pl.ds(at, step)] = raised
            return total + raised

        keep_total(
            lax.fori_loop(0, keys // step, raise_part, jnp.zeros((rows, step), jnp.float32))
        )

    share = 1.0 / total_ref[...]
    def weigh(j, sums):
        at = pl.multiple_of(j * 2816, 2816)
        probs = e_scr[:, pl.ds(at, 2816)] * jnp.tile(share, (1, 2816 // 128))
        return sums + jnp.dot(
            probs.astype(jnp.bfloat16),
            kv_all[pl.ds(at, 2816), :],
            preferred_element_type=jnp.float32,
        )

    sums = lax.fori_loop(0, keys // 2816, weigh, jnp.zeros((rows, 2 * HD), jnp.float32))
    for block in range(CHIPS):
        top = sums[block * HD : block * HD + HD // 2, :]
        bottom = sums[block * HD + HD // 2 : (block + 1) * HD, :]
        joined = jnp.where(lane < HD, pltpu.roll(top, HD, 1), bottom)
        out_ref[spots[2 + pl.program_id(0) * CHIPS + block]] = joined.astype(jnp.bfloat16)


def attended_rows(spots, branch, own_pieces, other_pieces, prepared, cache, text, earlier):
    pieces = (*own_pieces, *other_pieces)
    rows = sum(piece.shape[0] for piece in own_pieces)
    patch = 2 * rows
    keys = prepared[0].shape[1] + patch

    def whole(part):
        return pl.BlockSpec(part.shape, lambda i, spots: (0, 0))

    out_shape = (
        jax.ShapeDtypeStruct((2 * CHIPS, HD, 2 * HD), jnp.bfloat16),
        jax.ShapeDtypeStruct((2, patch, 2 * HD), jnp.bfloat16),
    )
    out_specs = (
        pl.BlockSpec((2 * CHIPS, HD // 2, 2 * HD), lambda i, spots: (0, branch, 0)),
        pl.BlockSpec((None, patch, 2 * HD), lambda i, spots: (branch, 0, 0)),
    )
    anywhere = pl.BlockSpec(memory_space=pl.ANY)
    return pl.pallas_call(
        functools.partial(attend_kernel, (len(own_pieces), len(other_pieces)), branch),
        out_shape=out_shape,
        grid_spec=pltpu.PrefetchScalarGridSpec(
            num_scalar_prefetch=1,
            grid=(2,),
            in_specs=[whole(part) for part in pieces]
            + [anywhere, pl.BlockSpec((None, 1, 2 * HD), lambda i, spots: (branch, 0, 0))]
            + [anywhere] * (2 + len(earlier)),
            out_specs=out_specs,
            scratch_shapes=[
                pltpu.VMEM((keys, 4 * HD), jnp.bfloat16),
                pltpu.VMEM((keys, 2 * HD), jnp.bfloat16),
                pltpu.VMEM((rows, 4 * HD), jnp.bfloat16),
                pltpu.VMEM((rows, keys), jnp.float32),
                pltpu.VMEM((rows, 2 * HD), jnp.float32),
                pltpu.VMEM((1, 2 * HD), jnp.float32),
                pltpu.SemaphoreType.DMA((5,)),
            ],
        ),
        input_output_aliases={1 + len(pieces) + 4 + i: i for i in range(len(earlier))},
        compiler_params=pltpu.CompilerParams(vmem_limit_bytes=48 * MIB),
        cost_estimate=pl.CostEstimate(
            flops=4 * patch * keys * 256, bytes_accessed=8 * MIB, transcendentals=0
        ),
    )(spots, *pieces, *prepared, cache, text, *earlier)


def finish_kernel(columns, heads, weight, entering, gate, out_ref, lhs):
    rows = entering.shape[1]
    lane = lax.broadcasted_iota(jnp.int32, (1, 2 * HD), 1)
    for pair in range(CHIPS):
        low = heads[2 * pair].astype(jnp.float32)
        high = heads[2 * pair + 1].astype(jnp.float32)
        top = jnp.where(lane < HD, low, pltpu.roll(high, HD, 1)).astype(jnp.bfloat16)
        bottom = jnp.where(lane < HD, pltpu.roll(low, HD, 1), high).astype(jnp.bfloat16)
        here = slice(pair * 2 * HD, (pair + 1) * 2 * HD)
        for branch in range(2):
            to = branch * rows
            part = slice(branch * rows // 2, (branch + 1) * rows // 2)
            lhs[to : to + rows // 2, here] = top[part]
            lhs[to + rows // 2 : to + rows, here] = bottom[part]
    sums = jnp.dot(lhs[...], weight[:, columns], preferred_element_type=jnp.float32)
    for branch in range(2):
        part = sums[branch * rows : (branch + 1) * rows]
        out_ref[branch] = (
            entering[branch, :, columns].astype(jnp.float32) + gate[2:3, columns] * part
        ).astype(jnp.bfloat16)


def finished_rows(heads, weight, entering, mod_rows, columns):
    branches, rows = entering.shape[:2]
    width = columns.stop - columns.start
    return pl.pallas_call(
        functools.partial(finish_kernel, columns),
        out_shape=jax.ShapeDtypeStruct((branches, rows, width), jnp.bfloat16),
        scratch_shapes=[pltpu.VMEM((branches * rows, weight.shape[0]), jnp.bfloat16)],
        compiler_params=pltpu.CompilerParams(vmem_limit_bytes=24 * MIB),
        cost_estimate=pl.CostEstimate(
            flops=4 * rows * width * weight.shape[0],
            bytes_accessed=weight.shape[0] * width * 2,
            transcendentals=0,
        ),
    )(heads, weight, entering, mod_rows)


def local(
    patch_in,
    modulation,
    qkv_weight,
    qk_gain,
    out_weight,
    kv_cache,
    text_kv,
    patch_offsets,
    step_index,
    text_count,
):
    entering = patch_in[0]
    mod_rows = modulation[0]
    def first_round(rows):
        return [rows] + [along(rows, 0, step) for step in STEPS[1:]]

    line = first_round(normed_rows(entering, 0, mod_rows))

    patch_offsets, step_index, text_count = after(
        (patch_offsets, step_index, text_count), line[0]
    )
    section_index = lax.axis_index("section")
    place = lax.axis_index("seq")
    core = place % 2
    x = (place // 2) % SIDE
    z = place // (2 * SIDE)
    patch_total = patch_offsets.shape[0]
    patch_number = (step_index[0] - section_index) % patch_total
    offset = jnp.sum(
        jnp.where(jnp.arange(patch_total, dtype=jnp.int32) == patch_number, patch_offsets, 0)
    )
    steps = jnp.array(STEPS, jnp.int32)
    outer = jnp.repeat(steps, SIDE)
    inner = jnp.tile(steps, SIDE)

    def chips_of(side):
        down = jnp.where(side == 0, outer, inner)
        across = jnp.where(side == 0, inner, outer)
        return ((z - down) % SIDE) * SIDE + (x - across) % SIDE

    fresh_places = jnp.concatenate(
        [chips_of(core) * 2 + core, chips_of(1 - core) * 2 + (1 - core)]
    )
    patch_rows = kv_cache.shape[2] // patch_total
    spots = jnp.concatenate([text_count, fresh_places, (offset // patch_rows)[None]])
    spots = spots.astype(jnp.int32)
    line_1 = first_round(normed_rows(after(entering, offset), 1, mod_rows))
    low, high = joined_rows(line)
    low, high, spots = lax.optimization_barrier((low, high, spots))
    left_low = along(low, 1, 1)
    right_high = along(high, 1, -1)
    left_high = along(high, 1, 1)
    right_low = along(low, 1, -1)
    cache, text, qkv_weight, qk_gain = after((kv_cache[0], text_kv[0], qkv_weight, qk_gain), low)
    weight = qkv_weight[0].T
    packed_weight = packed_rows(weight, swapped(weight))
    gains = jnp.pad(qk_gain[0], ((0, 0), (0, HD)), constant_values=1.0)
    prepared = prepared_keys(spots, cache, text)
    left_low, right_high, prepared, packed_weight, gains = lax.optimization_barrier(
        (left_low, right_high, prepared, packed_weight, gains)
    )

    def project(pieces):
        own, other = projected_rows(pieces, packed_weight, gains)
        return own, swapped(other)

    far_low = along(left_low, 1, 1)
    far_high = along(right_high, 1, -1)
    own_near, other_near = project([low, high, left_low, left_high, right_low, right_high])
    line_1 = after(jnp.concatenate(line_1, axis=0), far_low, far_high)
    left_1 = along(line_1, 1, 1)
    right_1 = along(line_1, 1, -1)
    far_1 = along(line_1, 1, 2)
    own_far, other_far = project([far_low, far_high])
    first = attended_rows(
        spots, 0, (own_near, own_far), (other_near, other_far), prepared, cache, text, ()
    )
    left_1, right_1, far_1, first = lax.optimization_barrier((left_1, right_1, far_1, first))
    own_all, other_all = project([line_1, left_1, right_1, far_1])
    attended, fresh = attended_rows(
        spots, 1, (own_all,), (other_all,), prepared, cache, text, first
    )

    heads = lax.all_to_all(attended, "seq", split_axis=0, concat_axis=0, tiled=True)
    count = lax.axis_size("section")
    width = entering.shape[2]
    cut = width // 256 * 128 + 128
    moved = []
    for columns in (slice(0, cut), slice(cut, width)):
        done = finished_rows(heads, out_weight[0], entering, mod_rows, columns)
        moved.append(lax.ppermute(done, "section", [(i, (i + 1) % count) for i in range(count)]))
    moved = jnp.concatenate(moved, axis=-1)
    return (moved[None], fresh[None])


def solution(mesh):
    in_specs = (
        P("section", None, "seq", None),
        P("section", None, None),
        P("section", None, "seq"),
        P("section", None, None),
        P("section", None, None),
        P("section", None, None, "seq"),
        P("section", None, None, "seq"),
        P(),
        P(),
        P(),
    )
    out_specs = (P("section", None, "seq", None), P("section", None, None, "seq"))
    return jax.shard_map(local, mesh=mesh, in_specs=in_specs, out_specs=out_specs, check_vma=False)
```
